512 devices in a mesh: expert: 64 (over z, y), dp: 8 (over x, core).
Axes of the slice: x: 4, y: 8, z: 8, core: 2. Of those that a mesh axis runs over, the one named last changes fastest.
Arguments:
- tokens: bfloat16 [1024, 4096], P('expert', 'dp'), may hold values from -6 to 6
- expert_ids: int32 [1024, 8], P('expert'), may hold values from 0 to 63, as said below
- route_weight: float32 [1024, 8], P('expert'), may hold values from 0.05 to 0.5
- placement: int32 [4], replicated, may hold values from 0 to 63, as said below
- gate_up_base: bfloat16 [64, 4096, 2048], P('expert', 'dp'), may hold values from -0.09375 to 0.09375
- down_base: bfloat16 [64, 1024, 4096], P('expert', None, 'dp'), may hold values from -0.1875 to 0.1875
- gate_up_a: bfloat16 [64, 4096, 128], P('expert', 'dp'), may hold values from -0.09375 to 0.09375
- gate_up_b: bfloat16 [64, 128, 1024], P('expert'), may hold values from -0.75 to 0.75
- down_a: bfloat16 [64, 1024, 64], P('expert'), may hold values from -0.1875 to 0.1875
- down_b: bfloat16 [64, 64, 4096], P('expert', None, 'dp'), may hold values from -0.75 to 0.75
- grad_mixed: bfloat16 [1024, 4096], P('expert', 'dp'), may hold values from -6 to 6
Outputs:
- mixed: bfloat16 [1024, 4096], P('expert', 'dp')
- grad_tokens: bfloat16 [1024, 4096], P('expert', 'dp')
- grad_gate_up_a: float32 [64, 4096, 128], P('expert', 'dp')
- grad_gate_up_b: float32 [64, 128, 1024], P('expert')
- grad_down_a: float32 [64, 1024, 64], P('expert')
- grad_down_b: float32 [64, 64, 4096], P('expert', None, 'dp')
- column_rows: int32 [64], P('expert')
- column_blocks: int32 [64], P('expert')
The draws below stay inside these ranges and needn't reach their ends.
Inputs may be any that keep to these rules, and one draw needn't show every extreme that they name: `expert_ids`: every device's 16 tokens name expert placement[0] exactly 8 times and each other expert at most 2 times; the 8 experts of one token are distinct. placement[0] is the hot expert; the other 3 entries are distinct indices of the expert axis, none equal to placement[0]; index 63 is always among the entries.
All inputs are finite; a program needn't handle non-finite values.
Results may differ from the reference program's by a relative error of at most 0.03.
Values may be sent and summed in bfloat16 or wider, within the bound.
A program may use at most 64 MiB of HBM per device.

```python
import math
import jax
import jax.numpy as jnp
from jax import lax

D = 4096
EXPERT_HIDDEN = 1024
ADAPTER_RANK = 64
TOPK = 8
COPIES = 3
TOK_COL = 16
EXPERTS = 64
TOKENS = 1024
HOT_ROWS = 8
OTHER_ROWS = 2
N_DP = 8


def shared_hot(key):
    hot_expert = jax.random.randint(jax.random.fold_in(key, 101), (), 0, EXPERTS)
    others = jax.random.permutation(jax.random.fold_in(key, 102), EXPERTS - 1)[:COPIES]
    replica_cols = (hot_expert + 1 + others) % EXPERTS
    last_index = EXPERTS - 1
    present = (hot_expert == last_index) | jnp.any(replica_cols == last_index)
    chosen_slot = jax.random.randint(jax.random.fold_in(key, 103), (), 0, COPIES)
    replace_here = jnp.logical_and(jnp.logical_not(present), jnp.arange(COPIES) == chosen_slot)
    replica_cols = jnp.where(replace_here, last_index, replica_cols)
    return (hot_expert, replica_cols)


def draw_placement(key, part):
    hot_expert, replica_cols = shared_hot(key)
    return jnp.concatenate([hot_expert[None], replica_cols]).astype(jnp.int32)


def draw_expert_ids(key, part):
    hot_expert, replica_cols = shared_hot(key)
    key = jax.random.fold_in(key, 7)

    def one_column(column_key):
        first_key, second_key, third_key = jax.random.split(column_key, 3)
        others = (hot_expert + 1 + jax.random.permutation(first_key, EXPERTS - 1)) % EXPERTS
        token_pos = jnp.arange(TOK_COL)[:, None]
        slot_pos = jnp.arange(TOPK)[None, :]
        hot_token = token_pos < HOT_ROWS
        start_pos = hot_token.astype(jnp.int32)
        rank_pos = token_pos * TOPK - jnp.minimum(token_pos, HOT_ROWS) + slot_pos - start_pos
        chosen = jnp.where(hot_token & (slot_pos == 0), hot_expert, others[rank_pos % (EXPERTS - 1)])
        chosen = chosen[jax.random.permutation(second_key, TOK_COL)]
        slot_keys = jax.random.split(third_key, TOK_COL)
        slot_perm = jax.vmap(lambda single_key: jax.random.permutation(single_key, TOPK))(slot_keys)
        return jnp.take_along_axis(chosen, slot_perm, axis=1)
    column_keys = jax.random.split(key, EXPERTS)
    return jax.vmap(one_column)(column_keys).reshape(TOKENS, TOPK).astype(jnp.int32)


def level_of(own_key, shape, shards, least, top_value):
    def one(axis_at, parts):
        heights = jax.random.uniform(jax.random.fold_in(jax.random.fold_in(own_key, 6), axis_at), (parts,), jnp.float32, least / len(shards), top_value / len(shards))
        return jnp.repeat(jnp.exp(heights), shape[axis_at] // parts).reshape((-1,) + (1,) * (len(shape) - axis_at - 1))

    level = one(*shards[0])
    for cut in shards[1:]:
        level = level * one(*cut)
    return level


def noise(own_key, extent, scale, most, cuts=(), kind=jnp.bfloat16):
    result = jax.random.normal(own_key, extent, jnp.float32) * scale
    if len(cuts) > 0:
        result = level_of(own_key, extent, cuts, -0.22, 0.18) * result
    return jnp.clip(result, min=-most, max=most).astype(kind)


def setup_inputs(seed: int = 0) -> dict:
    splits = jax.random.split(jax.random.key(seed), 12)
    tokens = noise(splits[0], (TOKENS, D), 1.0, 6.0, ((0, 64), (1, 8)))
    expert_ids = draw_expert_ids(jax.random.fold_in(splits[11], 71), 0)
    route_weight = jnp.clip(jnp.exp(math.log(0.5) - 2.3025851 * jax.random.uniform(splits[2], (TOKENS, TOPK), jnp.float32) ** level_of(splits[2], (TOKENS, TOPK), ((0, 64),), -0.2, 0.2)), 0.05, 0.5)
    placement = draw_placement(jax.random.fold_in(splits[11], 71), 0)
    gate_up_base = noise(splits[4], (EXPERTS, D, 2 * EXPERT_HIDDEN), D ** -0.5, 0.09375, ((0, 64), (1, 8)))
    down_base = noise(splits[5], (EXPERTS, EXPERT_HIDDEN, D), EXPERT_HIDDEN ** -0.5, 0.1875, ((0, 64), (2, 8)))
    gate_up_a = noise(splits[6], (EXPERTS, D, 2 * ADAPTER_RANK), D ** -0.5, 0.09375, ((0, 64), (1, 8)))
    gate_up_b = noise(splits[7], (EXPERTS, 2 * ADAPTER_RANK, EXPERT_HIDDEN), ADAPTER_RANK ** -0.5, 0.75, ((0, 64),))
    down_a = noise(splits[8], (EXPERTS, EXPERT_HIDDEN, ADAPTER_RANK), EXPERT_HIDDEN ** -0.5, 0.1875, ((0, 64),))
    down_b = noise(splits[9], (EXPERTS, ADAPTER_RANK, D), ADAPTER_RANK ** -0.5, 0.75, ((0, 64), (2, 8)))
    grad_mixed = noise(splits[10], (TOKENS, D), 1.0, 6.0, ((0, 64), (1, 8)))
    return dict(tokens=tokens, expert_ids=expert_ids, route_weight=route_weight, placement=placement, gate_up_base=gate_up_base, down_base=down_base, gate_up_a=gate_up_a, gate_up_b=gate_up_b, down_a=down_a, down_b=down_b, grad_mixed=grad_mixed)


adapter_scale = 0.25


def slice_sum(left_split, right_split, form):
    terms = jnp.einsum(form, left_split.astype(jnp.float32), right_split.astype(jnp.float32), precision=lax.Precision.HIGHEST)
    terms = lax.optimization_barrier(terms.astype(jnp.bfloat16))
    return jnp.sum(terms.astype(jnp.float32), 0)


def trailing_product(left, right):
    return lax.dot_general(left, right, (((1,), (1,)), ((), ())), preferred_element_type=jnp.float32)


def leading_product(left, right):
    return lax.dot_general(left, right, (((0,), (0,)), ((), ())), preferred_element_type=jnp.float32)


def expert_pass(row_features, slot_gradient_rows, weights):
    frozen_gate_up_weight, frozen_down_weight, lowrank_input, lowrank_output, down_adapter_input, down_adapter_output = weights
    count = row_features.shape[0]
    slice_width = D // N_DP
    rows_split = row_features.reshape(count, N_DP, slice_width)
    reduced_sum = slice_sum(rows_split, frozen_gate_up_weight.reshape(N_DP, slice_width, 2 * EXPERT_HIDDEN), "rpd,pdf->prf")
    lowrank_value = slice_sum(rows_split, lowrank_input.reshape(N_DP, slice_width, 2 * ADAPTER_RANK), "rpd,pdf->prf").astype(jnp.bfloat16)
    gate_activation = reduced_sum[:, :EXPERT_HIDDEN] + adapter_scale * jnp.dot(lowrank_value[:, :ADAPTER_RANK], lowrank_output[:ADAPTER_RANK], preferred_element_type=jnp.float32)
    up_projection_value = reduced_sum[:, EXPERT_HIDDEN:] + adapter_scale * jnp.dot(lowrank_value[:, ADAPTER_RANK:], lowrank_output[ADAPTER_RANK:], preferred_element_type=jnp.float32)
    sigmoid_gate = jax.nn.sigmoid(gate_activation)
    activated = gate_activation * sigmoid_gate
    hidden_activation = (activated * up_projection_value).astype(jnp.bfloat16)
    hidden_lowrank = jnp.dot(hidden_activation, down_adapter_input, preferred_element_type=jnp.float32).astype(jnp.bfloat16)
    layer_output = (jnp.dot(hidden_activation, frozen_down_weight, preferred_element_type=jnp.float32) + adapter_scale * jnp.dot(hidden_lowrank, down_adapter_output, preferred_element_type=jnp.float32)).astype(jnp.bfloat16)
    grads_split = slot_gradient_rows.reshape(count, N_DP, slice_width)
    backward_total = slice_sum(grads_split, frozen_down_weight.reshape(EXPERT_HIDDEN, N_DP, slice_width), "rpd,fpd->prf")
    backward_lowrank = slice_sum(grads_split, down_adapter_output.reshape(ADAPTER_RANK, N_DP, slice_width), "rpd,fpd->prf").astype(jnp.bfloat16)
    gradient_hidden_units = backward_total + adapter_scale * trailing_product(backward_lowrank, down_adapter_input)
    gradient_down_adapter_output = adapter_scale * leading_product(hidden_lowrank, slot_gradient_rows)
    gradient_down_adapter_input = adapter_scale * leading_product(hidden_activation, backward_lowrank)
    grad_gate = gradient_hidden_units * up_projection_value * sigmoid_gate * (1.0 + gate_activation * (1.0 - sigmoid_gate))
    grad_up = gradient_hidden_units * activated
    gradient_gate_up_pair = jnp.concatenate([grad_gate, grad_up], 1).astype(jnp.bfloat16)
    gradient_lowrank_output = adapter_scale * jnp.concatenate([leading_product(lowrank_value[:, :ADAPTER_RANK], gradient_gate_up_pair[:, :EXPERT_HIDDEN]), leading_product(lowrank_value[:, ADAPTER_RANK:], gradient_gate_up_pair[:, EXPERT_HIDDEN:])], 0)
    lowrank_backward = jnp.concatenate([trailing_product(gradient_gate_up_pair[:, :EXPERT_HIDDEN], lowrank_output[:ADAPTER_RANK]), trailing_product(gradient_gate_up_pair[:, EXPERT_HIDDEN:], lowrank_output[ADAPTER_RANK:])], 1).astype(jnp.bfloat16)
    gradient_lowrank_input = adapter_scale * leading_product(row_features, lowrank_backward)
    gradient_row_block = (trailing_product(gradient_gate_up_pair, frozen_gate_up_weight) + adapter_scale * trailing_product(lowrank_backward, lowrank_input)).astype(jnp.bfloat16)
    return layer_output, gradient_row_block, gradient_lowrank_input, gradient_lowrank_output, gradient_down_adapter_input, gradient_down_adapter_output


def reference(tokens, expert_ids, route_weight, placement, gate_up_base, down_base, gate_up_a, gate_up_b, down_a, down_b, grad_mixed):
    slot_count = TOKENS * TOPK
    flat_ids = expert_ids.reshape(-1).astype(jnp.int32)
    hot_expert = placement[0]
    is_hot = flat_ids == hot_expert
    columns = jnp.arange(EXPERTS, dtype=jnp.int32)
    onehot = ((flat_ids[:, None] == columns[None, :]) & (~is_hot)[:, None]).astype(jnp.int32)
    rank_other = jnp.sum((jnp.cumsum(onehot, 0) - 1) * onehot, 1).astype(jnp.int32)
    slot_index = jnp.arange(slot_count, dtype=jnp.int32)
    target_row = jnp.where(is_hot, EXPERTS, flat_ids).astype(jnp.int32)
    table = jnp.full((EXPERTS, EXPERTS * OTHER_ROWS), slot_count, jnp.int32).at[target_row, rank_other].set(slot_index, mode="drop")
    rank_hot = (jnp.cumsum(is_hot.astype(jnp.int32)) - 1).astype(jnp.int32)
    hot_place = jnp.where(is_hot, rank_hot, EXPERTS * HOT_ROWS).astype(jnp.int32)
    hot_table = jnp.full((EXPERTS * HOT_ROWS,), slot_count, jnp.int32).at[hot_place].set(slot_index, mode="drop")
    token_pad = jnp.concatenate([tokens, jnp.zeros((1, D), jnp.bfloat16)], 0)
    slot_grad = (route_weight[:, :, None] * grad_mixed[:, None, :].astype(jnp.float32)).astype(jnp.bfloat16).reshape(slot_count, D)
    grad_pad = jnp.concatenate([slot_grad, jnp.zeros((1, D), jnp.bfloat16)], 0)

    def one_expert(packed):
        index_row = packed[0]
        row_features = token_pad[index_row // TOPK]
        return expert_pass(row_features, grad_pad[index_row], packed[1:])

    main_out = lax.map(one_expert, (table, gate_up_base, down_base, gate_up_a, gate_up_b, down_a, down_b))
    hot_weights = (gate_up_base[hot_expert], down_base[hot_expert], gate_up_a[hot_expert], gate_up_b[hot_expert], down_a[hot_expert], down_b[hot_expert])
    hot_out = expert_pass(token_pad[hot_table // TOPK], grad_pad[hot_table], hot_weights)
    flat_table = table.reshape(-1)
    out_slots = jnp.zeros((slot_count + 1, D), jnp.bfloat16).at[flat_table].set(main_out[0].reshape(-1, D)).at[hot_table].set(hot_out[0])
    back_slots = jnp.zeros((slot_count + 1, D), jnp.bfloat16).at[flat_table].set(main_out[1].reshape(-1, D)).at[hot_table].set(hot_out[1])
    weighted = route_weight[:, :, None] * out_slots[:slot_count].reshape(TOKENS, TOPK, D).astype(jnp.float32)
    mixed = jnp.sum(weighted, 1).astype(jnp.bfloat16)
    grad_tokens = jnp.sum(back_slots[:slot_count].reshape(TOKENS, TOPK, D).astype(jnp.float32), 1).astype(jnp.bfloat16)
    grad_gate_up_a = main_out[2].at[hot_expert].add(hot_out[2])
    grad_gate_up_b = main_out[3].at[hot_expert].add(hot_out[3])
    grad_down_a = main_out[4].at[hot_expert].add(hot_out[4])
    grad_down_b = main_out[5].at[hot_expert].add(hot_out[5])
    source_col = jnp.arange(TOKENS, dtype=jnp.int32) // TOK_COL
    host_col = placement[(source_col * (COPIES + 1)) // EXPERTS]
    destination = jnp.where(expert_ids == hot_expert, host_col[:, None], expert_ids)
    counts = jnp.sum((destination[:, :, None] == columns[None, None, :]).astype(jnp.int32), (0, 1)).astype(jnp.int32)
    column_blocks = ((counts + 127) // 128).astype(jnp.int32)
    return mixed, grad_tokens, grad_gate_up_a, grad_gate_up_b, grad_down_a, grad_down_b, counts, column_blocks
```

```python
import jax
import jax.numpy as jnp
from jax import lax
from jax.experimental import pallas as pl
from jax.experimental.pallas import tpu as pltpu
from jax.sharding import PartitionSpec as P

SCALE = 0.25
BF = jnp.bfloat16
F32 = jnp.float32
NY, NZ, NX = 8, 8, 4
COLS = NY * NZ
TOK = 16
DF = 512
HID = 1024
PARTS = 5
ROWS = 128
BLK = 16
LANE = 128
C_LOW, C_BACK, C_BL, WP = 2048, 2176, 3200, 3328
HALF = 1664
A_GB, A_LB, A_LOW, A_HB, WA = 1024, 3072, 3200, 3328, 3456
AHALF = 1792
HW = 640
TICKS = PARTS + 6


def dot(a, b):
    return jnp.dot(a, b, preferred_element_type=F32)


def dot_t(a, b):
    return lax.dot_general(a, b, (((1,), (1,)), ((), ())), preferred_element_type=F32)


def t_dot(a, b):
    return lax.dot_general(a, b, (((0,), (0,)), ((), ())), preferred_element_type=F32)


def kernel(
    tok, ids, rw, grad, plc, gu_h, dn_h, ga_h, gb_h, da_h, db_h,
    mixed_o, gtok_o, gga_o, ggb_o, gda_o, gdb_o, rows_o, blocks_o,
    gu, dn, ga, gb, da, db, wsem,
    route, hroute, stage, nsend, nrecv, nback, nret, hg, xs, gs, pt, pr, ss, ra, rb, ag,
    hret, hgot, ysend, ygot,
    s_n, r_n, s_b, r_b, s_y, r_y, s_zp, r_zp, s_zm, r_zm, s_h, r_h, s_w, r_w,
    s_pair, r_pair, s_rs, r_2a, r_2b, s_ag, r_agx, r_fwd, s_core, r_core,
):
    e = lax.axis_index("expert")
    d = lax.axis_index("dp")
    z, y = e // NY, e % NY
    x, c = d // 2, d % 2

    def push(src, dst, ssem, rsem, dev):
        pltpu.make_async_remote_copy(
            src_ref=src, dst_ref=dst, send_sem=ssem, recv_sem=rsem, device_id=dev,
            device_id_type=pl.DeviceIdType.MESH,
        ).start()

    def wait(ref, sem):
        pltpu.make_async_copy(ref, ref, sem).wait()

    loads = [
        pltpu.make_async_copy(src, dst, wsem.at[i])
        for i, (src, dst) in enumerate(
            ((gu_h, gu), (dn_h, dn), (ga_h, ga), (gb_h, gb), (da_h, da), (db_h, db.at[0:64]))
        )
    ]
    for load in loads:
        load.start()

    xp = ((x + 1) % NX) * 2 + c
    xm = ((x + NX - 1) % NX) * 2 + c
    mate = x * 2 + (1 - c)

    barrier = pltpu.get_barrier_semaphore()

    def greet(i, carry):
        pl.semaphore_signal(
            barrier, inc=1, device_id=((e + i) % COLS, d), device_id_type=pl.DeviceIdType.MESH
        )
        return carry

    lax.fori_loop(1, COLS, greet, 0)
    for peer in (xp, xm, mate):
        pl.semaphore_signal(
            barrier, inc=1, device_id=(e, peer), device_id_type=pl.DeviceIdType.MESH
        )

    db[64:128, :] = jnp.zeros((64, DF), BF)

    hot = plc[0]
    is_hot = (hot == e).astype(F32)
    lane = lax.broadcasted_iota(jnp.int32, (TOK, LANE), 1)
    member = jnp.zeros((TOK, LANE), F32)
    weight = jnp.zeros((TOK, LANE), F32)
    for k in range(ids.shape[1]):
        same = ids[:, k : k + 1] == lane
        member = member + jnp.where(same, 1.0, 0.0)
        weight = weight + jnp.where(same, rw[:, k : k + 1], 0.0)
    row_i = lax.broadcasted_iota(jnp.int32, (TOK, TOK), 0)
    col_i = lax.broadcasted_iota(jnp.int32, (TOK, TOK), 1)
    before = jnp.where(row_i > col_i, 1.0, 0.0).astype(BF)
    rank = dot(before, member.astype(BF))
    hot_lane = jnp.where(lane == hot, 1.0, 0.0)
    cold = member * (1.0 - hot_lane)
    tokens = tok[...]
    grads = grad[...]
    ones = jnp.ones((TOK, DF), F32)
    for r in range(2):
        pick = jnp.where(rank == r, cold, 0.0)
        route[r] = pick
        route[2 + r] = pick * weight
        xr = t_dot(pick.astype(BF), tokens)
        gr = t_dot(pick.astype(BF), grads)
        wr = lax.dot_general(
            pick * weight, ones, (((0,), (0,)), ((), ())),
            precision=lax.Precision.HIGHEST, preferred_element_type=F32,
        )
        for q in range(4):
            cut = slice(q * LANE, (q + 1) * LANE)
            stage[pl.ds(r * 4 + q, COLS, stride=16), :] = xr[:COLS, cut]
            stage[pl.ds(8 + r * 4 + q, COLS, stride=16), :] = gr[:COLS, cut] * wr[:COLS, cut]
    nsend[...] = stage[...].astype(BF).reshape(COLS, 16, LANE)

    hm = jnp.sum(member * hot_lane, axis=1, keepdims=True)
    hw = jnp.sum(weight * hot_lane, axis=1, keepdims=True)
    hr = jnp.sum(rank * hot_lane, axis=1, keepdims=True)
    hpick = jnp.where(lane.astype(F32) == hr, hm, 0.0)
    hroute[0] = hpick
    hroute[1] = hpick * hw
    hx = t_dot(hpick.astype(BF), tokens)[0:8]
    hgr = t_dot(hpick.astype(BF), (hw * grads.astype(F32)).astype(BF))[0:8]
    count = jnp.broadcast_to(jnp.sum(member, axis=0, keepdims=True), (16, LANE))
    hg[z, y, :, 0:DF] = jnp.concatenate([hx, hgr], axis=0).astype(BF)
    hg[z, y, :, DF:HW] = count.astype(BF)

    pl.semaphore_wait(barrier, COLS - 1 + 3)

    for o in range(1, NY):
        push(hg.at[z, y], hg.at[z, y], s_y, r_y, (z * NY + (y + o) % NY, d))

    def send_n(i, carry):
        to = (e + i) % COLS
        push(nsend.at[to], nrecv.at[e], s_n, r_n, (to, d))
        return carry

    lax.fori_loop(1, COLS, send_n, 0)
    nrecv[e] = nsend[e]
    zp = ((z + 1) % NZ) * NY + y
    zm = ((z + NZ - 1) % NZ) * NY + y

    def ring_send(s):
        at = (z + NZ - s) % NZ
        push(hg.at[at], hg.at[at], s_zp.at[s], r_zp.at[s], (zp, d))

        @pl.when(s < 3)
        def _():
            am = (z + s) % NZ
            push(hg.at[am], hg.at[am], s_zm.at[s], r_zm.at[s], (zm, d))

    wait(hg.at[z, pl.ds(0, NY - 1)], r_y)
    ring_send(0)
    for load in loads:
        load.wait()

    def offset(p, i):
        first = p % 4 + 1
        return first if i == 0 else (8 - first) - 4 * (first // 4)

    def partial(p):
        xv = xs[p]
        gv = gs[p]

        def one(n, carry):
            at = pl.ds(pl.multiple_of(n * 512, 512), 512)
            pt[p, :, at] = dot(xv, gu[:, at]).astype(BF)
            return carry

        lax.fori_loop(0, 4, one, 0)
        pt[p, :, C_LOW:C_BACK] = dot(xv, ga[...]).astype(BF)
        for n in range(2):
            pt[p, :, C_BACK + n * 512 : C_BACK + (n + 1) * 512] = dot_t(
                gv, dn[n * 512 : (n + 1) * 512, :]
            ).astype(BF)
        pt[p, :, C_BL:WP] = dot_t(gv, db[...]).astype(BF)
        push(
            pt.at[p, pl.ds(pl.multiple_of((1 - c) * 64, 64), 64)], pr.at[p],
            s_pair.at[p], r_pair.at[p], (e, mate),
        )

    def rows_of(xx):
        return pl.ds(pl.multiple_of((xx % NX) * BLK, BLK), BLK)

    def block_of(core, xx):
        return pl.ds(pl.multiple_of((core * NX + xx % NX) * BLK, BLK), BLK)

    def tick(t, carry):
        @pl.when((t >= 6) & (t < 6 + PARTS))
        def _():
            p = t - 6
            wait(ag.at[p, pl.ds(0, 64)], r_core.at[p])
            hid = ag[p, :, 0:HID]
            hb = ag[p, :, A_HB:WA]
            out = dot(hid, dn[...]) + SCALE * dot(hb, db[...])
            both = ag[p, :, A_GB:A_LB]
            lb = ag[p, :, A_LB:A_LOW]
            dx = dot_t(both, gu[...]) + SCALE * dot_t(lb, ga[...])

            @pl.when(p == 0)
            def _():
                for r in range(2):
                    for q in range(4):
                        cut = slice(q * LANE, (q + 1) * LANE)
                        rs = slice(r * COLS, (r + 1) * COLS)
                        stage[pl.ds(r * 4 + q, COLS, stride=16), :] = out[rs, cut]
                        stage[pl.ds(8 + r * 4 + q, COLS, stride=16), :] = dx[rs, cut]
                nback[...] = stage[...].astype(BF).reshape(COLS, 16, LANE)

                def send_b(i, carry):
                    to = (e + i) % COLS
                    push(nback.at[to], nret.at[e], s_b, r_b, (to, d))
                    return carry

                lax.fori_loop(1, COLS, send_b, 0)
                nret[e] = nback[e]

            @pl.when(p > 0)
            def _():
                for i in range(2):
                    o = offset(p, i)
                    rs = slice(i * 64, (i + 1) * 64)
                    block = jnp.concatenate(
                        [out[rs].reshape(NY, 8, DF), dx[rs].reshape(NY, 8, DF)], axis=1
                    )
                    hret[o] = block.astype(BF)

                    @pl.when(o > 0)
                    def _():
                        push(
                            hret.at[o], hgot.at[o], s_h, r_h.at[o],
                            (((z + o) % NZ) * NY + y, d),
                        )

        @pl.when((t >= 5) & (t < 5 + PARTS))
        def _():
            p = t - 5
            far = block_of(c, x + 2)
            wait(ag.at[p, far, pl.ds(0, AHALF)], r_fwd.at[p, 0])
            wait(ag.at[p, far, pl.ds(AHALF, WA - AHALF)], r_fwd.at[p, 1])
            push(ag.at[p, far], ag.at[p, far], s_core.at[p], r_core.at[p], (e, mate))

        @pl.when((t >= 4) & (t < 4 + PARTS))
        def _():
            p = t - 4
            left = block_of(c, x + NX - 1)
            right = block_of(c, x + 1)
            lo = pl.ds(0, AHALF)
            hi = pl.ds(AHALF, WA - AHALF)
            wait(ag.at[p, left], r_agx.at[p, 0])
            push(ag.at[p, left, lo], ag.at[p, left, lo], s_ag.at[p], r_fwd.at[p, 0], (e, xp))
            push(ag.at[p, left], ag.at[p, left], s_core.at[p], r_core.at[p], (e, mate))
            wait(ag.at[p, right], r_agx.at[p, 1])
            push(ag.at[p, right, hi], ag.at[p, right, hi], s_ag.at[p], r_fwd.at[p, 1], (e, xm))
            push(ag.at[p, right], ag.at[p, right], s_core.at[p], r_core.at[p], (e, mate))

        @pl.when((t >= 3) & (t < 3 + PARTS))
        def _():
            p = t - 3
            wait(rb.at[p, 0], r_2b.at[p, 0])
            wait(rb.at[p, 1], r_2b.at[p, 1])
            own = rows_of(x)

            def total(lo, hi):
                return (
                    ss[p, own, lo:hi].astype(F32)
                    + rb[p, 0, :, lo:hi].astype(F32)
                    + rb[p, 1, :, lo:hi].astype(F32)
                )

            low = total(C_LOW, C_BACK).astype(BF)
            bl = total(C_BL, WP).astype(BF)
            left_half = lax.broadcasted_iota(jnp.int32, (BLK, LANE), 1) < 64
            low32 = low.astype(F32)
            low_g = jnp.where(left_half, low32, 0.0).astype(BF)
            low_u = jnp.where(left_half, 0.0, low32).astype(BF)
            gate = total(0, HID) + SCALE * dot(low_g, gb[...])
            up = total(HID, C_LOW) + SCALE * dot(low_u, gb[...])
            gh = total(C_BACK, C_BL) + SCALE * dot_t(bl[:, 0:64], da[...])
            sig = jax.nn.sigmoid(gate)
            act = gate * sig
            hidden = (act * up).astype(BF)
            gg = (gh * up * sig * (1.0 + gate * (1.0 - sig))).astype(BF)
            gup = (gh * act).astype(BF)
            hl = dot(hidden, da[...])
            lb = jnp.where(left_half, dot_t(gg, gb[...]), dot_t(gup, gb[...]))
            mine = block_of(c, x)
            ag[p, mine, 0:HID] = hidden
            ag[p, mine, HID : 2 * HID] = gg
            ag[p, mine, 2 * HID : A_LB] = gup
            ag[p, mine, A_LB:A_LOW] = lb.astype(BF)
            ag[p, mine, A_LOW:A_HB] = low
            ag[p, mine, A_HB:WA] = jnp.concatenate(
                [hl, bl[:, 0:64].astype(F32)], axis=1
            ).astype(BF)
            here = ag.at[p, mine]
            push(here, here, s_ag.at[p], r_agx.at[p, 0], (e, xp))
            push(here, here, s_ag.at[p], r_agx.at[p, 1], (e, xm))
            push(here, here, s_core.at[p], r_core.at[p], (e, mate))

        @pl.when((t >= 2) & (t < 2 + PARTS))
        def _():
            p = t - 2
            right = rows_of(x + 1)
            left = rows_of(x + NX - 1)
            wait(ra.at[p, 0], r_2a.at[p, 0])
            ss[p, right, 0:HALF] = (
                ss[p, right, 0:HALF].astype(F32) + ra[p, 0].astype(F32)
            ).astype(BF)
            push(ss.at[p, right], rb.at[p, 0], s_rs.at[p], r_2b.at[p, 0], (e, xp))
            wait(ra.at[p, 1], r_2a.at[p, 1])
            ss[p, left, HALF:WP] = (
                ss[p, left, HALF:WP].astype(F32) + ra[p, 1].astype(F32)
            ).astype(BF)
            push(ss.at[p, left], rb.at[p, 1], s_rs.at[p], r_2b.at[p, 1], (e, xm))

        @pl.when((t >= 1) & (t < 1 + PARTS))
        def _():
            p = t - 1
            wait(pr.at[p], r_pair.at[p])

            def add(i, carry):
                xx = (x + 2 + i) % NX
                mine = block_of(c, xx)
                at = rows_of(xx)
                ss[p, at, :] = (pt[p, mine, :].astype(F32) + pr[p, at, :].astype(F32)).astype(BF)

                @pl.when(i == 0)
                def _():
                    push(
                        ss.at[p, at, pl.ds(0, HALF)], ra.at[p, 0],
                        s_rs.at[p], r_2a.at[p, 0], (e, xp),
                    )
                    push(
                        ss.at[p, at, pl.ds(HALF, HALF)], ra.at[p, 1],
                        s_rs.at[p], r_2a.at[p, 1], (e, xm),
                    )

                return carry

            lax.fori_loop(0, NX, add, 0)

        @pl.when(t == 0)
        def _():
            wait(nrecv.at[pl.ds(0, COLS - 1)], r_n)
            stage[...] = nrecv[...].reshape(COLS * 16, LANE).astype(F32)
            for r in range(2):
                for q in range(4):
                    cut = slice(q * LANE, (q + 1) * LANE)
                    rs = slice(r * COLS, (r + 1) * COLS)
                    xs[0, rs, cut] = stage[pl.ds(r * 4 + q, COLS, stride=16), :].astype(BF)
                    gs[0, rs, cut] = stage[pl.ds(8 + r * 4 + q, COLS, stride=16), :].astype(BF)

        @pl.when(t < 4)
        def _():
            wait(hg.at[0], r_zp.at[t])

            @pl.when(t < 3)
            def _():
                wait(hg.at[0], r_zm.at[t])
                ring_send(t + 1)

        @pl.when((t >= 1) & (t < PARTS))
        def _():
            for i in range(2):
                plane = (z + offset(t, i)) % NZ
                v = hg[plane, :, :, 0:DF].astype(F32) * is_hot
                rs = slice(i * 64, (i + 1) * 64)
                xs[t, rs, :] = v[:, 0:8, :].reshape(64, DF).astype(BF)
                gs[t, rs, :] = v[:, 8:16, :].reshape(64, DF).astype(BF)

        @pl.when(t < PARTS)
        def _():
            partial(t)

        return carry

    lax.fori_loop(0, TICKS, tick, 0)

    for o in range(1, NZ):
        wait(hgot.at[o], r_h.at[o])
    got = hret[0].astype(F32)
    for o in range(1, NZ):
        got = got + hgot[o].astype(F32)
    ysend[...] = got.astype(BF)
    for o in range(1, NY):
        to = (y + o) % NY
        push(ysend.at[to], ygot.at[o], s_w, r_w, (z * NY + to, d))
    ygot[0] = ysend[y]

    xall = xs[...].reshape(PARTS * ROWS, DF)
    gall = gs[...].reshape(PARTS * ROWS, DF)

    def cols(lo, hi):
        return ag[:, :, lo:hi].reshape(PARTS * ROWS, hi - lo)

    gga_o[...] = SCALE * t_dot(cols(A_LB, A_LOW), xall).T
    hb = cols(A_HB, WA)
    low = cols(A_LOW, A_HB)
    ggb_o[0:64, :] = SCALE * t_dot(low, cols(A_GB, A_GB + HID))[0:64]
    ggb_o[64:128, :] = SCALE * t_dot(low, cols(A_GB + HID, A_LB))[64:128]
    gda_o[...] = SCALE * t_dot(hb, cols(0, HID))[64:128].T
    gdb_o[...] = SCALE * t_dot(hb, gall)[0:64]

    total = jnp.sum(
        hg[:, :, :, DF:HW].astype(F32).reshape(COLS * 16, LANE), axis=0, keepdims=True
    )
    lane1 = lax.broadcasted_iota(jnp.int32, (1, LANE), 1)
    mine = jnp.sum(jnp.where(lane1 == e, total, 0.0)) * (1.0 / 16.0)
    held = (plc[0] == e) | (plc[1] == e) | (plc[2] == e) | (plc[3] == e)
    share = COLS // 4 * 8
    rows = jnp.where(hot == e, 0, mine.astype(jnp.int32)) + jnp.where(held, share, 0)
    rows_o[0] = rows
    blocks_o[0] = (rows + 127) // 128

    wait(nret.at[pl.ds(0, COLS - 1)], r_b)
    stage[...] = nret[...].reshape(COLS * 16, LANE).astype(F32)
    wait(ygot.at[pl.ds(1, NY - 1)], r_w)
    back = ygot[0].astype(F32)
    for o in range(1, NY):
        back = back + ygot[o].astype(F32)

    def exact(a, b):
        return jnp.dot(a, b, precision=lax.Precision.HIGHEST, preferred_element_type=F32)

    hpick = hroute[0][:, 0:8]
    hpw = hroute[1][:, 0:8]
    for q in range(4):
        cut = slice(q * LANE, (q + 1) * LANE)
        mix = exact(hpw, back[0:8, cut])
        gt = exact(hpick, back[8:16, cut])
        for r in range(2):
            mix = mix + exact(route[2 + r][:, 0:COLS], stage[pl.ds(r * 4 + q, COLS, stride=16), :])
            gt = gt + dot(
                route[r][:, 0:COLS].astype(BF),
                stage[pl.ds(8 + r * 4 + q, COLS, stride=16), :].astype(BF),
            )
        mixed_o[:, cut] = mix.astype(BF)
        gtok_o[:, cut] = gt.astype(BF)

    wait(nsend.at[pl.ds(0, COLS - 1)], s_n)
    wait(nback.at[pl.ds(0, COLS - 1)], s_b)
    wait(hg.at[0, pl.ds(0, NY - 1)], s_y)
    for s in range(4):
        wait(hg.at[0], s_zp.at[s])
    for s in range(3):
        wait(hg.at[0], s_zm.at[s])
    wait(hret.at[pl.ds(1, NZ - 1)], s_h)
    wait(ysend.at[pl.ds(0, NY - 1)], s_w)
    for p in range(PARTS):
        wait(pt.at[p, pl.ds(0, 64)], s_pair.at[p])
        wait(ss.at[p, pl.ds(0, 48)], s_rs.at[p])
        wait(ag.at[p, pl.ds(0, 48)], s_ag.at[p])
        wait(ag.at[p, pl.ds(0, 64)], s_core.at[p])


def per_device(
    tokens, expert_ids, route_weight, placement, gate_up_base, down_base, gate_up_a, gate_up_b,
    down_a, down_b, grad_mixed,
):
    vmem = pl.BlockSpec(memory_space=pltpu.VMEM)
    smem = pl.BlockSpec(memory_space=pltpu.SMEM)
    hbm = pl.BlockSpec(memory_space=pl.ANY)
    dma = pltpu.SemaphoreType.DMA
    out = pl.pallas_call(
        kernel,
        out_shape=(
            jax.ShapeDtypeStruct((TOK, DF), BF),
            jax.ShapeDtypeStruct((TOK, DF), BF),
            jax.ShapeDtypeStruct((DF, 128), F32),
            jax.ShapeDtypeStruct((128, HID), F32),
            jax.ShapeDtypeStruct((HID, 64), F32),
            jax.ShapeDtypeStruct((64, DF), F32),
            jax.ShapeDtypeStruct((1,), jnp.int32),
            jax.ShapeDtypeStruct((1,), jnp.int32),
        ),
        in_specs=[vmem] * 4 + [smem] + [hbm] * 6,
        out_specs=[vmem] * 6 + [smem] * 2,
        scratch_shapes=[
            pltpu.VMEM((DF, 2 * HID), BF),
            pltpu.VMEM((HID, DF), BF),
            pltpu.VMEM((DF, 128), BF),
            pltpu.VMEM((128, HID), BF),
            pltpu.VMEM((HID, 64), BF),
            pltpu.VMEM((128, DF), BF),
            dma((6,)),
            pltpu.VMEM((4, TOK, LANE), F32),
            pltpu.VMEM((2, TOK, LANE), F32),
            pltpu.VMEM((COLS * 16, LANE), F32),
            pltpu.VMEM((COLS, 16, LANE), BF),
            pltpu.VMEM((COLS, 16, LANE), BF),
            pltpu.VMEM((COLS, 16, LANE), BF),
            pltpu.VMEM((COLS, 16, LANE), BF),
            pltpu.VMEM((NZ, NY, 16, HW), BF),
            pltpu.VMEM((PARTS, ROWS, DF), BF),
            pltpu.VMEM((PARTS, ROWS, DF), BF),
            pltpu.VMEM((PARTS, ROWS, WP), BF),
            pltpu.VMEM((PARTS, 64, WP), BF),
            pltpu.VMEM((PARTS, 64, WP), BF),
            pltpu.VMEM((PARTS, 2, BLK, HALF), BF),
            pltpu.VMEM((PARTS, 2, BLK, WP), BF),
            pltpu.VMEM((PARTS, ROWS, WA), BF),
            pltpu.VMEM((NZ, NY, 16, DF), BF),
            pltpu.VMEM((NZ, NY, 16, DF), BF),
            pltpu.VMEM((NY, 16, DF), BF),
            pltpu.VMEM((NY, 16, DF), BF),
            dma, dma, dma, dma, dma, dma,
            dma((4,)), dma((4,)), dma((3,)), dma((3,)),
            dma, dma((NZ,)), dma, dma,
            dma((PARTS,)), dma((PARTS,)),
            dma((PARTS,)), dma((PARTS, 2)), dma((PARTS, 2)),
            dma((PARTS,)), dma((PARTS, 2)), dma((PARTS, 2)),
            dma((PARTS,)), dma((PARTS,)),
        ],
        compiler_params=pltpu.CompilerParams(
            collective_id=0, has_side_effects=True, vmem_limit_bytes=56 * 1024 * 1024
        ),
    )(
        tokens, expert_ids, route_weight, grad_mixed, placement, gate_up_base[0], down_base[0],
        gate_up_a[0], gate_up_b[0], down_a[0], down_b[0],
    )
    mixed, gtok, gga, ggb, gda, gdb, rows, blocks = out
    return mixed, gtok, gga[None], ggb[None], gda[None], gdb[None], rows, blocks


def solution(mesh):
    return jax.shard_map(
        per_device,
        mesh=mesh,
        in_specs=(
            P("expert", "dp"),
            P("expert", None),
            P("expert", None),
            P(),
            P("expert", "dp", None),
            P("expert", None, "dp"),
            P("expert", "dp", None),
            P("expert", None, None),
            P("expert", None, None),
            P("expert", None, "dp"),
            P("expert", "dp"),
        ),
        out_specs=(
            P("expert", "dp"),
            P("expert", "dp"),
            P("expert", "dp", None),
            P("expert", None, None),
            P("expert", None, None),
            P("expert", None, "dp"),
            P("expert"),
            P("expert"),
        ),
        check_vma=False,
    )
```

```python
import jax
import jax.numpy as jnp
from jax import lax
from jax.experimental import pallas as pl
from jax.experimental.pallas import tpu as pltpu
from jax.sharding import PartitionSpec as P

SCALE = 0.25
BF = jnp.bfloat16
F32 = jnp.float32
NY, NZ, NX = 8, 8, 4
COLS = NY * NZ
TOK = 16
DF = 512
HID = 1024
PARTS = 4
ROWS = 128
BLK = 16
LANE = 128
C_LOW, C_BACK, C_BL, WP = 2048, 2176, 3200, 3328
HALF = 1664
A_GB, A_LB, A_LOW, A_HB, WA = 1024, 3072, 3200, 3328, 3456
AHALF = 1792
CUT = 256
TICKS = PARTS + 6


def dot(a, b):
    return jnp.dot(a, b, preferred_element_type=F32)


def dot_t(a, b):
    return lax.dot_general(a, b, (((1,), (1,)), ((), ())), preferred_element_type=F32)


def t_dot(a, b):
    return lax.dot_general(a, b, (((0,), (0,)), ((), ())), preferred_element_type=F32)


def kernel(
    tok, ids, rw, grad, plc, gu_h, dn_h, ga_h, gb_h, da_h, db_h,
    mixed_o, gtok_o, gga_o, ggb_o, gda_o, gdb_o, rows_o, blocks_o,
    gu, dn, ga, gb, da, db, wsem,
    route, hroute, stage, nsend, nrecv, nback, nret, hg, xs, gs, pt, pr, ss, ra, rb, ag,
    hret, hgot_a, hgot_b, ysend, ygot, zsend, zgot,
    cy, cz, s_n, r_n, s_b, r_b, s_y, r_y, s_zp, r_zp, s_zm, r_zm,
    s_cy, r_cy, s_cz, r_cz, s_ha, r_ha, s_hb, r_hb, s_w, r_w, s_v, r_v,
    s_pair, r_pair, s_rs, r_2a, r_2b, s_ag, r_agx, r_fwd, s_core, r_core,
):
    e = lax.axis_index("expert")
    d = lax.axis_index("dp")
    z, y = e // NY, e % NY
    x, c = d // 2, d % 2

    def push(src, dst, ssem, rsem, dev):
        pltpu.make_async_remote_copy(
            src_ref=src, dst_ref=dst, send_sem=ssem, recv_sem=rsem, device_id=dev,
            device_id_type=pl.DeviceIdType.MESH,
        ).start()

    def wait(ref, sem):
        pltpu.make_async_copy(ref, ref, sem).wait()

    xp = ((x + 1) % NX) * 2 + c
    xm = ((x + NX - 1) % NX) * 2 + c
    mate = x * 2 + (1 - c)

    barrier = pltpu.get_barrier_semaphore()

    def greet(i, carry):
        pl.semaphore_signal(
            barrier, inc=1, device_id=((e + i) % COLS, d), device_id_type=pl.DeviceIdType.MESH
        )
        return carry

    lax.fori_loop(1, COLS, greet, 0)
    for peer in (xp, xm, mate):
        pl.semaphore_signal(
            barrier, inc=1, device_id=(e, peer), device_id_type=pl.DeviceIdType.MESH
        )

    loads = [
        pltpu.make_async_copy(src, dst, wsem.at[i])
        for i, (src, dst) in enumerate(
            ((gu_h, gu), (dn_h, dn), (ga_h, ga), (gb_h, gb), (da_h, da), (db_h, db.at[0:64]))
        )
    ]
    for load in loads:
        load.start()

    db[64:128, :] = jnp.zeros((64, DF), BF)

    hot = plc[0]
    is_hot = (hot == e).astype(F32)
    expert = lax.broadcasted_iota(jnp.int32, (LANE, TOK), 0)
    member = jnp.zeros((LANE, TOK), F32)
    weight = jnp.zeros((LANE, TOK), F32)
    for k in range(ids.shape[0]):
        same = ids[k : k + 1, :] == expert
        member = member + jnp.where(same, 1.0, 0.0)
        weight = weight + jnp.where(same, rw[k : k + 1, :], 0.0)
    row_i = lax.broadcasted_iota(jnp.int32, (TOK, TOK), 0)
    col_i = lax.broadcasted_iota(jnp.int32, (TOK, TOK), 1)
    before = jnp.where(row_i < col_i, 1.0, 0.0).astype(BF)
    rank = dot(member.astype(BF), before)
    hot_row = jnp.where(expert == hot, 1.0, 0.0)
    cold = member * (1.0 - hot_row)
    tokens = tok[...]
    grads = grad[...]
    for r in range(2):
        pick = jnp.where(rank == r, cold, 0.0)[0:COLS]
        pw = pick * weight[0:COLS]
        route[r] = pick
        route[2 + r] = pw
        xr = dot(pick.astype(BF), tokens)
        gr = dot(pick.astype(BF), grads) * jnp.sum(pw, axis=1, keepdims=True)
        for q in range(4):
            cut = slice(q * LANE, (q + 1) * LANE)
            stage[pl.ds(r * 4 + q, COLS, stride=16), :] = xr[:, cut]
            stage[pl.ds(8 + r * 4 + q, COLS, stride=16), :] = gr[:, cut]
    nsend[...] = stage[...].astype(BF).reshape(COLS, 16, LANE)

    hm = jnp.sum(member * hot_row, axis=0, keepdims=True)
    hw = jnp.sum(weight * hot_row, axis=0, keepdims=True)
    hr = jnp.sum(rank * hot_row, axis=0, keepdims=True)
    place = lax.broadcasted_iota(jnp.int32, (8, TOK), 0).astype(F32)
    hpick = jnp.where(place == hr, hm, 0.0)
    hpw = hpick * hw
    hroute[0] = hpick
    hroute[1] = hpw
    hx = dot(hpick.astype(BF), tokens)
    hgr = dot(hpick.astype(BF), grads) * jnp.sum(hpw, axis=1, keepdims=True)
    hg[z, y] = jnp.concatenate([hx, hgr], axis=0).astype(BF)
    cy[0] = dot_t(jnp.ones((16, TOK), BF), member.astype(BF)).astype(BF)

    pl.semaphore_wait(barrier, COLS - 1 + 3)

    lo, hi = pl.ds(0, CUT), pl.ds(CUT, DF - CUT)
    for o in range(1, NY):
        push(hg.at[z, y], hg.at[z, y], s_y, r_y, (z * NY + (y + o) % NY, d))
    for o in range(1, NY):
        push(cy.at[0], cy.at[o], s_cy, r_cy, (z * NY + (y + o) % NY, d))

    def send_n(i, carry):
        to = (e + i) % COLS
        push(nsend.at[to], nrecv.at[e], s_n, r_n, (to, d))
        return carry

    lax.fori_loop(1, COLS, send_n, 0)
    nrecv[e] = nsend[e]
    zp = ((z + 1) % NZ) * NY + y
    zm = ((z + NZ - 1) % NZ) * NY + y
    rows16 = pl.ds(0, 16)

    def plane_half(at, h):
        return hg.at[at % NZ, pl.ds(0, NY), rows16, (lo, hi)[h]]

    def ring_send(s, h):
        up = plane_half(z + NZ - s, h)
        push(up, up, s_zp.at[s, h], r_zp.at[s, h], (zp, d))
        if s < 3:
            down = plane_half(z + s, h)
            push(down, down, s_zm.at[s, h], r_zm.at[s, h], (zm, d))

    def ring_wait(s):
        for h in range(2):
            wait(plane_half(0, h), r_zp.at[s, h])
            if s < 3:
                wait(plane_half(0, h), r_zm.at[s, h])
                ring_send(s + 1, h)

    wait(hg.at[z, pl.ds(0, NY - 1)], r_y)
    ring_send(0, 0)
    ring_send(0, 1)
    wait(cy.at[pl.ds(0, NY - 1)], r_cy)
    count = cy[0].astype(F32)
    for o in range(1, NY):
        count = count + cy[o].astype(F32)
    cz[0] = count.astype(BF)
    for o in range(1, NZ):
        push(cz.at[0], cz.at[o], s_cz, r_cz, (((z + o) % NZ) * NY + y, d))
    for load in loads:
        load.wait()

    def offset(p, i):
        first = (p + 2) * ((p + 2) // 3) - 3 * (p // 3)
        return first if i == 0 else (9 - first) % NZ

    def hot_rows(p, i):
        v = hg[(z + offset(p, i)) % NZ].astype(F32) * is_hot
        return v[:, 0:8, :].reshape(64, DF), v[:, 8:16, :].reshape(64, DF)

    def partial(p):
        xv = xs[p]
        gv = gs[p]

        def one(n, carry):
            at = pl.ds(pl.multiple_of(n * 512, 512), 512)
            pt[p, :, at] = dot(xv, gu[:, at]).astype(BF)
            return carry

        lax.fori_loop(0, 4, one, 0)
        pt[p, :, C_LOW:C_BACK] = dot(xv, ga[...]).astype(BF)
        for n in range(2):
            pt[p, :, C_BACK + n * 512 : C_BACK + (n + 1) * 512] = dot_t(
                gv, dn[n * 512 : (n + 1) * 512, :]
            ).astype(BF)
        pt[p, :, C_BL:WP] = dot_t(gv, db[...]).astype(BF)
        push(
            pt.at[p, pl.ds(pl.multiple_of((1 - c) * 64, 64), 64)], pr.at[p],
            s_pair.at[p], r_pair.at[p], (e, mate),
        )

    def rows_of(xx):
        return pl.ds(pl.multiple_of((xx % NX) * BLK, BLK), BLK)

    def block_of(core, xx):
        return pl.ds(pl.multiple_of((core * NX + xx % NX) * BLK, BLK), BLK)

    def tick(t, carry):
        @pl.when((t >= 6) & (t < 6 + PARTS))
        def _():
            p = t - 6
            wait(ag.at[p, pl.ds(0, 64)], r_core.at[p])
            hid = ag[p, :, 0:HID]
            hb = ag[p, :, A_HB:WA]
            out = dot(hid, dn[...]) + SCALE * dot(hb, db[...])
            both = ag[p, :, A_GB:A_LB]
            lb = ag[p, :, A_LB:A_LOW]
            dx = dot_t(both, gu[...]) + SCALE * dot_t(lb, ga[...])

            @pl.when(p == 0)
            def _():
                for r in range(2):
                    for q in range(4):
                        cut = slice(q * LANE, (q + 1) * LANE)
                        rs = slice(r * COLS, (r + 1) * COLS)
                        stage[pl.ds(r * 4 + q, COLS, stride=16), :] = out[rs, cut]
                        stage[pl.ds(8 + r * 4 + q, COLS, stride=16), :] = dx[rs, cut]
                nback[...] = stage[...].astype(BF).reshape(COLS, 16, LANE)

                def send_b(i, carry):
                    to = (e + i) % COLS
                    push(nback.at[to], nret.at[e], s_b, r_b, (to, d))
                    return carry

                lax.fori_loop(1, COLS, send_b, 0)
                nret[e] = nback[e]

            for i in range(2):
                o = offset(p, i)
                rs = slice(i * 64, (i + 1) * 64)
                block = jnp.concatenate(
                    [out[rs].reshape(NY, 8, DF), dx[rs].reshape(NY, 8, DF)], axis=1
                )
                hret[o] = (block * is_hot).astype(BF)
                for v in range(1, NY):
                    to = (y + v) % NY
                    push(
                        hret.at[o, to, rows16, hi], hgot_b.at[o, v], s_hb, r_hb.at[o],
                        (z * NY + to, d),
                    )

                @pl.when(o > 0)
                def _():
                    push(
                        hret.at[o, pl.ds(0, NY), rows16, lo], hgot_a.at[o], s_ha, r_ha.at[o],
                        (((z + o) % NZ) * NY + y, d),
                    )

        @pl.when((t >= 5) & (t < 5 + PARTS))
        def _():
            p = t - 5
            far = block_of(c, x + 2)
            wait(ag.at[p, far, pl.ds(0, AHALF)], r_fwd.at[p, 0])
            wait(ag.at[p, far, pl.ds(AHALF, WA - AHALF)], r_fwd.at[p, 1])
            push(ag.at[p, far], ag.at[p, far], s_core.at[p], r_core.at[p], (e, mate))

        @pl.when((t >= 4) & (t < 4 + PARTS))
        def _():
            p = t - 4
            left = block_of(c, x + NX - 1)
            right = block_of(c, x + 1)
            lo = pl.ds(0, AHALF)
            hi = pl.ds(AHALF, WA - AHALF)
            wait(ag.at[p, left], r_agx.at[p, 0])
            push(ag.at[p, left, lo], ag.at[p, left, lo], s_ag.at[p], r_fwd.at[p, 0], (e, xp))
            push(ag.at[p, left], ag.at[p, left], s_core.at[p], r_core.at[p], (e, mate))
            wait(ag.at[p, right], r_agx.at[p, 1])
            push(ag.at[p, right, hi], ag.at[p, right, hi], s_ag.at[p], r_fwd.at[p, 1], (e, xm))
            push(ag.at[p, right], ag.at[p, right], s_core.at[p], r_core.at[p], (e, mate))

        @pl.when((t >= 3) & (t < 3 + PARTS))
        def _():
            p = t - 3
            wait(rb.at[p, 0], r_2b.at[p, 0])
            wait(rb.at[p, 1], r_2b.at[p, 1])
            own = rows_of(x)

            def total(lo, hi):
                return (
                    ss[p, own, lo:hi].astype(F32)
                    + rb[p, 0, :, lo:hi].astype(F32)
                    + rb[p, 1, :, lo:hi].astype(F32)
                )

            low = total(C_LOW, C_BACK).astype(BF)
            bl = total(C_BL, WP).astype(BF)
            left_half = lax.broadcasted_iota(jnp.int32, (BLK, LANE), 1) < 64
            low32 = low.astype(F32)
            low_g = jnp.where(left_half, low32, 0.0).astype(BF)
            low_u = jnp.where(left_half, 0.0, low32).astype(BF)
            gate = total(0, HID) + SCALE * dot(low_g, gb[...])
            up = total(HID, C_LOW) + SCALE * dot(low_u, gb[...])
            gh = total(C_BACK, C_BL) + SCALE * dot(bl[:, 0:64], da[...])
            sig = jax.nn.sigmoid(gate)
            act = gate * sig
            hidden = (act * up).astype(BF)
            gg = (gh * up * sig * (1.0 + gate * (1.0 - sig))).astype(BF)
            gup = (gh * act).astype(BF)
            hl = dot_t(hidden, da[...])
            lb = jnp.where(left_half, dot_t(gg, gb[...]), dot_t(gup, gb[...]))
            mine = block_of(c, x)
            ag[p, mine, 0:HID] = hidden
            ag[p, mine, HID : 2 * HID] = gg
            ag[p, mine, 2 * HID : A_LB] = gup
            ag[p, mine, A_LB:A_LOW] = lb.astype(BF)
            ag[p, mine, A_LOW:A_HB] = low
            ag[p, mine, A_HB:WA] = jnp.concatenate(
                [hl, bl[:, 0:64].astype(F32)], axis=1
            ).astype(BF)
            here = ag.at[p, mine]
            push(here, here, s_ag.at[p], r_agx.at[p, 0], (e, xp))
            push(here, here, s_ag.at[p], r_agx.at[p, 1], (e, xm))
            push(here, here, s_core.at[p], r_core.at[p], (e, mate))

        @pl.when((t >= 2) & (t < 2 + PARTS))
        def _():
            p = t - 2
            right = rows_of(x + 1)
            left = rows_of(x + NX - 1)
            wait(ra.at[p, 0], r_2a.at[p, 0])
            ss[p, right, 0:HALF] = (
                ss[p, right, 0:HALF].astype(F32) + ra[p, 0].astype(F32)
            ).astype(BF)
            push(ss.at[p, right], rb.at[p, 0], s_rs.at[p], r_2b.at[p, 0], (e, xp))
            wait(ra.at[p, 1], r_2a.at[p, 1])
            ss[p, left, HALF:WP] = (
                ss[p, left, HALF:WP].astype(F32) + ra[p, 1].astype(F32)
            ).astype(BF)
            push(ss.at[p, left], rb.at[p, 1], s_rs.at[p], r_2b.at[p, 1], (e, xm))

        @pl.when((t >= 1) & (t < 1 + PARTS))
        def _():
            p = t - 1
            wait(pr.at[p], r_pair.at[p])

            def add(i, carry):
                xx = (x + 2 + i) % NX
                mine = block_of(c, xx)
                at = rows_of(xx)
                ss[p, at, :] = (pt[p, mine, :].astype(F32) + pr[p, at, :].astype(F32)).astype(BF)

                @pl.when(i == 0)
                def _():
                    push(
                        ss.at[p, at, pl.ds(0, HALF)], ra.at[p, 0],
                        s_rs.at[p], r_2a.at[p, 0], (e, xp),
                    )
                    push(
                        ss.at[p, at, pl.ds(HALF, HALF)], ra.at[p, 1],
                        s_rs.at[p], r_2a.at[p, 1], (e, xm),
                    )

                return carry

            lax.fori_loop(0, NX, add, 0)

        @pl.when(t == 0)
        def _():
            ring_wait(0)
            wait(nrecv.at[pl.ds(0, COLS - 1)], r_n)
            stage[...] = nrecv[...].reshape(COLS * 16, LANE).astype(F32)
            for r in range(2):
                for q in range(4):
                    cut = slice(q * LANE, (q + 1) * LANE)
                    rs = slice(r * COLS, (r + 1) * COLS)
                    xs[0, rs, cut] = stage[pl.ds(r * 4 + q, COLS, stride=16), :].astype(BF)
                    gs[0, rs, cut] = stage[pl.ds(8 + r * 4 + q, COLS, stride=16), :].astype(BF)

            for i in range(2):
                xv, gv = hot_rows(0, i)
                rs = slice(i * 64, (i + 1) * 64)
                xs[0, rs, :] = (xs[0, rs, :].astype(F32) + xv).astype(BF)
                gs[0, rs, :] = (gs[0, rs, :].astype(F32) + gv).astype(BF)

        @pl.when(t == 1)
        def _():
            ring_wait(1)
            ring_wait(2)

        @pl.when(t == 2)
        def _():
            ring_wait(3)

        @pl.when((t >= 1) & (t < PARTS))
        def _():
            for i in range(2):
                xv, gv = hot_rows(t, i)
                rs = slice(i * 64, (i + 1) * 64)
                xs[t, rs, :] = xv.astype(BF)
                gs[t, rs, :] = gv.astype(BF)

        @pl.when(t < PARTS)
        def _():
            partial(t)

        return carry

    lax.fori_loop(0, TICKS, tick, 0)

    for o in range(1, NZ):
        wait(hgot_a.at[o], r_ha.at[o])
    got = hret[0, :, :, 0:CUT].astype(F32)
    for o in range(1, NZ):
        got = got + hgot_a[o].astype(F32)
    ysend[...] = got.astype(BF)
    for v in range(1, NY):
        to = (y + v) % NY
        push(ysend.at[to], ygot.at[v], s_w, r_w, (z * NY + to, d))
    for o in range(NZ):
        wait(hgot_b.at[o, pl.ds(0, NY - 1)], r_hb.at[o])
        got = hret[o, y, :, CUT:DF].astype(F32)
        for v in range(1, NY):
            got = got + hgot_b[o, v].astype(F32)
        zsend[o] = got.astype(BF)
        if o > 0:
            push(zsend.at[o], zgot.at[o], s_v, r_v, (((z + o) % NZ) * NY + y, d))
    ygot[0] = ysend[y]
    zgot[0] = zsend[0]

    xall = xs[...].reshape(PARTS * ROWS, DF)
    gall = gs[...].reshape(PARTS * ROWS, DF)

    def cols(lo, hi):
        return ag[:, :, lo:hi].reshape(PARTS * ROWS, hi - lo)

    gga_o[...] = SCALE * t_dot(cols(A_LB, A_LOW), xall).T
    hb = cols(A_HB, WA)
    low = cols(A_LOW, A_HB)
    ggb_o[0:64, :] = SCALE * t_dot(low, cols(A_GB, A_GB + HID))[0:64]
    ggb_o[64:128, :] = SCALE * t_dot(low, cols(A_GB + HID, A_LB))[64:128]
    gda_o[...] = SCALE * t_dot(hb, cols(0, HID))[64:128]
    gdb_o[...] = SCALE * t_dot(hb, gall)[0:64]

    wait(cz.at[pl.ds(0, NZ - 1)], r_cz)
    total = jnp.sum(cz[...].astype(F32).reshape(NZ * 16, LANE), axis=0, keepdims=True)
    lane1 = lax.broadcasted_iota(jnp.int32, (1, LANE), 1)
    mine = jnp.sum(jnp.where(lane1 == e, total, 0.0)) * (1.0 / 16.0)
    held = (plc[0] == e) | (plc[1] == e) | (plc[2] == e) | (plc[3] == e)
    share = COLS // 4 * 8
    rows = jnp.where(hot == e, 0, mine.astype(jnp.int32)) + jnp.where(held, share, 0)
    rows_o[0] = rows
    blocks_o[0] = (rows + 127) // 128

    wait(nret.at[pl.ds(0, COLS - 1)], r_b)
    stage[...] = nret[...].reshape(COLS * 16, LANE).astype(F32)
    wait(ygot.at[pl.ds(1, NY - 1)], r_w)
    wait(zgot.at[pl.ds(1, NZ - 1)], r_v)
    back = [ygot[0].astype(F32), zgot[0].astype(F32)]
    for o in range(1, NY):
        back[0] = back[0] + ygot[o].astype(F32)
        back[1] = back[1] + zgot[o].astype(F32)

    def exact(a, b):
        return lax.dot_general(
            a, b, (((0,), (0,)), ((), ())),
            precision=lax.Precision.HIGHEST, preferred_element_type=F32,
        )

    for q in range(4):
        cut = slice(q * LANE, (q + 1) * LANE)
        half = back[q // 2][:, (q % 2) * LANE : (q % 2 + 1) * LANE]
        mix = exact(hroute[1], half[0:8])
        gt = exact(hroute[0], half[8:16])
        for r in range(2):
            mix = mix + exact(route[2 + r], stage[pl.ds(r * 4 + q, COLS, stride=16), :])
            gt = gt + t_dot(
                route[r].astype(BF), stage[pl.ds(8 + r * 4 + q, COLS, stride=16), :].astype(BF)
            )
        mixed_o[:, cut] = mix.astype(BF)
        gtok_o[:, cut] = gt.astype(BF)

    wait(nsend.at[pl.ds(0, COLS - 1)], s_n)
    wait(nback.at[pl.ds(0, COLS - 1)], s_b)
    wait(hg.at[z, pl.ds(0, NY - 1)], s_y)
    for h in range(2):
        for s in range(4):
            wait(plane_half(0, h), s_zp.at[s, h])
        for s in range(3):
            wait(plane_half(0, h), s_zm.at[s, h])
    wait(cy.at[pl.ds(0, NY - 1)], s_cy)
    wait(cz.at[pl.ds(0, NZ - 1)], s_cz)
    wait(hgot_a.at[pl.ds(1, NZ - 1)], s_ha)
    wait(hgot_b.at[pl.ds(0, NZ), pl.ds(0, NY - 1)], s_hb)
    wait(ysend.at[pl.ds(0, NY - 1)], s_w)
    wait(zsend.at[pl.ds(0, NZ - 1)], s_v)
    for p in range(PARTS):
        wait(pt.at[p, pl.ds(0, 64)], s_pair.at[p])
        wait(ss.at[p, pl.ds(0, 48)], s_rs.at[p])
        wait(ag.at[p, pl.ds(0, 48)], s_ag.at[p])
        wait(ag.at[p, pl.ds(0, 64)], s_core.at[p])


def copy_kernel(*refs):
    n = len(refs) // 2
    for i in range(n):
        refs[n + i][...] = refs[i][...]


def hand_over(arrays):
    vmem = pl.BlockSpec(memory_space=pltpu.VMEM)
    return pl.pallas_call(
        copy_kernel,
        out_shape=tuple(jax.ShapeDtypeStruct(a.shape, a.dtype) for a in arrays),
        in_specs=[vmem] * len(arrays),
        out_specs=tuple([vmem] * len(arrays)),
    )(*arrays)


def per_device(
    tokens, expert_ids, route_weight, placement, gate_up_base, down_base, gate_up_a, gate_up_b,
    down_a, down_b, grad_mixed,
):
    vmem = pl.BlockSpec(memory_space=pltpu.VMEM)
    smem = pl.BlockSpec(memory_space=pltpu.SMEM)
    hbm = pl.BlockSpec(memory_space=pl.ANY)
    dma = pltpu.SemaphoreType.DMA
    out = pl.pallas_call(
        kernel,
        out_shape=(
            jax.ShapeDtypeStruct((TOK, DF), BF),
            jax.ShapeDtypeStruct((TOK, DF), BF),
            jax.ShapeDtypeStruct((DF, 128), F32),
            jax.ShapeDtypeStruct((128, HID), F32),
            jax.ShapeDtypeStruct((64, HID), F32),
            jax.ShapeDtypeStruct((64, DF), F32),
            jax.ShapeDtypeStruct((1,), jnp.int32),
            jax.ShapeDtypeStruct((1,), jnp.int32),
        ),
        in_specs=[vmem] * 4 + [smem] + [hbm] * 6,
        out_specs=[vmem] * 6 + [smem] * 2,
        scratch_shapes=[
            pltpu.VMEM((DF, 2 * HID), BF),
            pltpu.VMEM((HID, DF), BF),
            pltpu.VMEM((DF, 128), BF),
            pltpu.VMEM((128, HID), BF),
            pltpu.VMEM((64, HID), BF),
            pltpu.VMEM((128, DF), BF),
            dma((6,)),
            pltpu.VMEM((4, COLS, TOK), F32),
            pltpu.VMEM((2, 8, TOK), F32),
            pltpu.VMEM((COLS * 16, LANE), F32),
            pltpu.VMEM((COLS, 16, LANE), BF),
            pltpu.VMEM((COLS, 16, LANE), BF),
            pltpu.VMEM((COLS, 16, LANE), BF),
            pltpu.VMEM((COLS, 16, LANE), BF),
            pltpu.VMEM((NZ, NY, 16, DF), BF),
            pltpu.VMEM((PARTS, ROWS, DF), BF),
            pltpu.VMEM((PARTS, ROWS, DF), BF),
            pltpu.VMEM((PARTS, ROWS, WP), BF),
            pltpu.VMEM((PARTS, 64, WP), BF),
            pltpu.VMEM((PARTS, 64, WP), BF),
            pltpu.VMEM((PARTS, 2, BLK, HALF), BF),
            pltpu.VMEM((PARTS, 2, BLK, WP), BF),
            pltpu.VMEM((PARTS, ROWS, WA), BF),
            pltpu.VMEM((NZ, NY, 16, DF), BF),
            pltpu.VMEM((NZ, NY, 16, CUT), BF),
            pltpu.VMEM((NZ, NY, 16, DF - CUT), BF),
            pltpu.VMEM((NY, 16, CUT), BF),
            pltpu.VMEM((NY, 16, CUT), BF),
            pltpu.VMEM((NZ, 16, DF - CUT), BF),
            pltpu.VMEM((NZ, 16, DF - CUT), BF),
            pltpu.VMEM((NY, 16, LANE), BF),
            pltpu.VMEM((NZ, 16, LANE), BF),
            dma, dma, dma, dma, dma, dma,
            dma((4, 2)), dma((4, 2)), dma((3, 2)), dma((3, 2)),
            dma, dma, dma, dma,
            dma, dma((NZ,)), dma, dma((NZ,)), dma, dma, dma, dma,
            dma((PARTS,)), dma((PARTS,)),
            dma((PARTS,)), dma((PARTS, 2)), dma((PARTS, 2)),
            dma((PARTS,)), dma((PARTS, 2)), dma((PARTS, 2)),
            dma((PARTS,)), dma((PARTS,)),
        ],
        compiler_params=pltpu.CompilerParams(
            collective_id=0, has_side_effects=True, vmem_limit_bytes=56 * 1024 * 1024
        ),
    )(
        tokens, expert_ids.T, route_weight.T, grad_mixed, placement, gate_up_base[0], down_base[0],
        gate_up_a[0], gate_up_b[0], down_a[0].T, down_b[0],
    )
    mixed, gtok, gga, ggb, gda, gdb = hand_over(out[:6])
    return mixed, gtok, gga[None], ggb[None], gda.T[None], gdb[None], out[6], out[7]


def solution(mesh):
    return jax.shard_map(
        per_device,
        mesh=mesh,
        in_specs=(
            P("expert", "dp"),
            P("expert", None),
            P("expert", None),
            P(),
            P("expert", "dp", None),
            P("expert", None, "dp"),
            P("expert", "dp", None),
            P("expert", None, None),
            P("expert", None, None),
            P("expert", None, "dp"),
            P("expert", "dp"),
        ),
        out_specs=(
            P("expert", "dp"),
            P("expert", "dp"),
            P("expert", "dp", None),
            P("expert", None, None),
            P("expert", None, None),
            P("expert", None, "dp"),
            P("expert"),
            P("expert"),
        ),
        check_vma=False,
    )
```

```python
import jax
import jax.numpy as jnp
from jax import lax
from jax.experimental import pallas as pl
from jax.experimental.pallas import tpu as pltpu
from jax.sharding import PartitionSpec as P

SCALE = 0.25
BF = jnp.bfloat16
F32 = jnp.float32
NY, NZ, NX = 8, 8, 4
COLS = NY * NZ
TOK = 16
DF = 512
HID = 1024
PARTS = 4
ROWS = 128
BLK = 16
LANE = 128
C_LOW, C_BACK, C_BL, WP = 2048, 2176, 3200, 3328
HALF = 1664
A_GB, A_LB, A_LOW, A_HB, WA = 1024, 3072, 3200, 3328, 3456
AHALF = 1792
CUT = 256
GAP, STEP = 1, 1
TICKS = GAP * (PARTS - 1) + 6 * STEP + 1


def dot(a, b):
    return jnp.dot(a, b, preferred_element_type=F32)


def dot_t(a, b):
    return lax.dot_general(a, b, (((1,), (1,)), ((), ())), preferred_element_type=F32)


def t_dot(a, b):
    return lax.dot_general(a, b, (((0,), (0,)), ((), ())), preferred_element_type=F32)


def kernel(
    tok, ids, rw, grad, plc, gu_h, dn_h, ga_h, gb_h, da_h, db_h,
    mixed_o, gtok_o, gga_o, ggb_o, gda_o, gdb_o, rows_o, blocks_o,
    gu, dn, ga, gb, da, db, wsem,
    route, hroute, stage, nsend, nmid, nrecv, nback, nhalf, nret, hg, xs, gs, pt, pr, ss, ra, rb, ag,
    hret, hgot_a, hgot_b, ysend, ygot, zsend, zgot,
    cy, cz, s_n, r_n, s_n2, r_n2, s_b, r_b, s_b2, r_b2, s_y, r_y, s_zp, r_zp, s_zm, r_zm,
    s_cy, r_cy, s_cz, r_cz, s_ha, r_ha, s_hb, r_hb, s_w, r_w, s_v, r_v,
    s_pair, r_pair, s_rs, r_2a, r_2b, s_ag, r_agx, r_fwd, s_core, r_core,
):
    e = lax.axis_index("expert")
    d = lax.axis_index("dp")
    z, y = e // NY, e % NY
    x, c = d // 2, d % 2

    def push(src, dst, ssem, rsem, dev):
        pltpu.make_async_remote_copy(
            src_ref=src, dst_ref=dst, send_sem=ssem, recv_sem=rsem, device_id=dev,
            device_id_type=pl.DeviceIdType.MESH,
        ).start()

    def wait(ref, sem):
        pltpu.make_async_copy(ref, ref, sem).wait()

    xp = ((x + 1) % NX) * 2 + c
    xm = ((x + NX - 1) % NX) * 2 + c
    mate = x * 2 + (1 - c)

    barrier = pltpu.get_barrier_semaphore()

    for o in range(1, NY):
        for peer in (z * NY + (y + o) % NY, ((z + o) % NZ) * NY + y):
            pl.semaphore_signal(
                barrier, inc=1, device_id=(peer, d), device_id_type=pl.DeviceIdType.MESH
            )
    for peer in (xp, xm, mate):
        pl.semaphore_signal(
            barrier, inc=1, device_id=(e, peer), device_id_type=pl.DeviceIdType.MESH
        )

    loads = [
        pltpu.make_async_copy(src, dst, wsem.at[i])
        for i, (src, dst) in enumerate(
            ((gu_h, gu), (dn_h, dn), (ga_h, ga), (gb_h, gb), (da_h, da), (db_h, db.at[0:64]))
        )
    ]
    for load in loads:
        load.start()

    db[64:128, :] = jnp.zeros((64, DF), BF)

    hot = plc[0]
    is_hot = (hot == e).astype(F32)
    row_i = lax.broadcasted_iota(jnp.int32, (TOK, TOK), 0)
    col_i = lax.broadcasted_iota(jnp.int32, (TOK, TOK), 1)
    before = jnp.where(row_i < col_i, 1.0, 0.0).astype(BF)

    def membership(expert):
        member = jnp.zeros(expert.shape, F32)
        weight = jnp.zeros(expert.shape, F32)
        for k in range(ids.shape[0]):
            same = ids[k : k + 1, :] == expert
            member = member + jnp.where(same, 1.0, 0.0)
            weight = weight + jnp.where(same, rw[k : k + 1, :], 0.0)
        return member, weight, dot(member.astype(BF), before)

    expert = lax.broadcasted_iota(jnp.int32, (LANE, TOK), 0)
    member, weight, rank = membership(expert)
    hot_row = jnp.where(expert == hot, 1.0, 0.0)
    tokens = tok[...]
    grads = grad[...]
    hm = jnp.sum(member * hot_row, axis=0, keepdims=True)
    hw = jnp.sum(weight * hot_row, axis=0, keepdims=True)
    hr = jnp.sum(rank * hot_row, axis=0, keepdims=True)
    place = lax.broadcasted_iota(jnp.int32, (8, TOK), 0).astype(F32)
    hpick = jnp.where(place == hr, hm, 0.0)
    hpw = hpick * hw
    hroute[0] = hpick.T
    hroute[1] = hpw.T
    hx = dot(hpick.astype(BF), tokens)
    hgr = dot(hpick.astype(BF), grads) * jnp.sum(hpw, axis=1, keepdims=True)
    hg[z, y] = jnp.concatenate([hx, hgr], axis=0).astype(BF)
    cy[0] = dot_t(jnp.ones((16, TOK), BF), member.astype(BF)).astype(BF)

    pl.semaphore_wait(barrier, NY - 1 + NZ - 1 + 3)

    lo, hi = pl.ds(0, CUT), pl.ds(CUT, DF - CUT)
    for o in range(1, NY):
        push(hg.at[z, y], hg.at[z, y], s_y, r_y, (z * NY + (y + o) % NY, d))
    for o in range(1, NY):
        push(cy.at[0], cy.at[o], s_cy, r_cy, (z * NY + (y + o) % NY, d))

    def keep(at, value):
        head = value.astype(BF)
        route[at] = head
        route[at + 1] = (value - head.astype(F32)).astype(BF)

    away = lax.broadcasted_iota(jnp.int32, (COLS, TOK), 0)
    there = ((z + (away >> 3)) & (NZ - 1)) * NY + ((y + (away & 7)) & (NY - 1))
    near, near_w, near_rank = membership(there)
    cold = jnp.where(there == hot, 0.0, near)
    for r in range(2):
        pick = jnp.where(near_rank == r, cold, 0.0)
        pw = pick * near_w
        route[r] = pick.astype(BF)
        keep(2 + 2 * r, pw)
        xr = dot(pick.astype(BF), tokens)
        gr = dot(pick.astype(BF), grads) * jnp.sum(pw, axis=1, keepdims=True)
        for q in range(4):
            cut = slice(q * LANE, (q + 1) * LANE)
            stage[pl.ds(r * 4 + q, COLS, stride=16), :] = xr[:, cut]
            stage[pl.ds(8 + r * 4 + q, COLS, stride=16), :] = gr[:, cut]
    nsend[...] = stage[...].astype(BF).reshape(NZ, NY, 16, LANE)
    for o in range(1, NZ):
        push(nsend.at[o], nmid.at[o], s_n, r_n, (((z + o) % NZ) * NY + y, d))
    nmid[0] = nsend[0]

    zp = ((z + 1) % NZ) * NY + y
    zm = ((z + NZ - 1) % NZ) * NY + y
    rows16 = pl.ds(0, 16)

    def plane_half(at, h):
        return hg.at[at % NZ, pl.ds(0, NY), rows16, (lo, hi)[h]]

    def ring_send(s, h):
        up = plane_half(z + NZ - s, h)
        push(up, up, s_zp.at[s, h], r_zp.at[s, h], (zp, d))
        if s < 3:
            down = plane_half(z + s, h)
            push(down, down, s_zm.at[s, h], r_zm.at[s, h], (zm, d))

    def ring_wait(s):
        for h in range(2):
            wait(plane_half(0, h), r_zp.at[s, h])
            if s < 3:
                wait(plane_half(0, h), r_zm.at[s, h])
                ring_send(s + 1, h)

    wait(hg.at[z, pl.ds(0, NY - 1)], r_y)
    ring_send(0, 0)
    ring_send(0, 1)

    wait(nmid.at[pl.ds(0, NZ - 1)], r_n)
    for o in range(1, NY):
        push(
            nmid.at[pl.ds(0, NZ), o], nrecv.at[pl.ds(0, NZ), o], s_n2, r_n2,
            (z * NY + (y + o) % NY, d),
        )
    nrecv[:, 0] = nmid[:, 0]
    wait(cy.at[pl.ds(0, NY - 1)], r_cy)
    count = cy[0].astype(F32)
    for o in range(1, NY):
        count = count + cy[o].astype(F32)
    cz[0] = count.astype(BF)
    for o in range(1, NZ):
        push(cz.at[0], cz.at[o], s_cz, r_cz, (((z + o) % NZ) * NY + y, d))
    for load in loads:
        load.wait()

    def offset(p, i):
        first = (p + 2) * ((p + 2) // 3) - 3 * (p // 3)
        return first if i == 0 else (9 - first) % NZ

    def hot_rows(p, i):
        v = hg[(z + offset(p, i)) % NZ].astype(F32) * is_hot
        return v[:, 0:8, :].reshape(64, DF), v[:, 8:16, :].reshape(64, DF)

    def partial(p):
        xv = xs[p]
        gv = gs[p]

        def one(n, carry):
            at = pl.ds(pl.multiple_of(n * 512, 512), 512)
            pt[p, :, at] = dot(xv, gu[:, at]).astype(BF)
            return carry

        lax.fori_loop(0, 4, one, 0)
        pt[p, :, C_LOW:C_BACK] = dot(xv, ga[...]).astype(BF)
        for n in range(2):
            pt[p, :, C_BACK + n * 512 : C_BACK + (n + 1) * 512] = dot_t(
                gv, dn[n * 512 : (n + 1) * 512, :]
            ).astype(BF)
        pt[p, :, C_BL:WP] = dot_t(gv, db[...]).astype(BF)
        push(
            pt.at[p, pl.ds(pl.multiple_of((1 - c) * 64, 64), 64)], pr.at[p],
            s_pair.at[p], r_pair.at[p], (e, mate),
        )

    def rows_of(xx):
        return pl.ds(pl.multiple_of((xx % NX) * BLK, BLK), BLK)

    def block_of(core, xx):
        return pl.ds(pl.multiple_of((core * NX + xx % NX) * BLK, BLK), BLK)

    def due(t, stage):
        since = t - stage * STEP
        return (since >= 0) & (since < GAP * PARTS) & ((since + 6 * STEP * GAP) % GAP == 0)

    first, second = pl.ds(0, HALF), pl.ds(HALF, HALF)

    def tick(t, carry):
        @pl.when(due(t, 6))
        def _():
            p = (t - 6 * STEP) // GAP
            wait(ag.at[p, pl.ds(0, 64)], r_core.at[p])
            hid = ag[p, :, 0:HID]
            hb = ag[p, :, A_HB:WA]
            out = dot(hid, dn[...]) + SCALE * dot(hb, db[...])
            both = ag[p, :, A_GB:A_LB]
            lb = ag[p, :, A_LB:A_LOW]
            dx = dot_t(both, gu[...]) + SCALE * dot_t(lb, ga[...])

            for i in range(2):
                o = offset(p, i)
                rs = slice(i * 64, (i + 1) * 64)
                block = jnp.concatenate(
                    [out[rs].reshape(NY, 8, DF), dx[rs].reshape(NY, 8, DF)], axis=1
                )
                hret[p, i] = (block * is_hot).astype(BF)

                @pl.when(o > 0)
                def _():
                    push(
                        hret.at[p, i, pl.ds(0, NY), rows16, lo], hgot_a.at[o], s_ha, r_ha.at[o],
                        (((z + o) % NZ) * NY + y, d),
                    )

            for v in range(1, NY):
                to = (y + v) % NY
                push(
                    hret.at[p, pl.ds(0, 2), to, rows16, hi], hgot_b.at[p, v], s_hb, r_hb.at[p],
                    (z * NY + to, d),
                )

            @pl.when(p == 1)
            def _():
                for r in range(2):
                    for q in range(4):
                        cut = slice(q * LANE, (q + 1) * LANE)
                        rs = slice(r * COLS, (r + 1) * COLS)
                        stage[pl.ds(r * 4 + q, COLS, stride=16), :] = out[rs, cut]
                        stage[pl.ds(8 + r * 4 + q, COLS, stride=16), :] = dx[rs, cut]
                nback[...] = stage[...].astype(BF).reshape(NZ, NY, 16, LANE)
                for v in range(1, NY):
                    push(
                        nback.at[pl.ds(0, NZ), v], nhalf.at[pl.ds(0, NZ), v], s_b, r_b,
                        (z * NY + (y + NY - v) % NY, d),
                    )
                nhalf[:, 0] = nback[:, 0]

        @pl.when(t == GAP + 6 * STEP + 2)
        def _():
            wait(nhalf.at[pl.ds(0, NZ), pl.ds(0, NY - 1)], r_b)
            for o in range(1, NZ):
                push(nhalf.at[o], nret.at[o], s_b2, r_b2, (((z + NZ - o) % NZ) * NY + y, d))
            nret[0] = nhalf[0]

        @pl.when(due(t, 5))
        def _():
            p = (t - 5 * STEP) // GAP
            far = block_of(c, x + 2)
            wait(ag.at[p, far, pl.ds(0, AHALF)], r_fwd.at[p, 0])
            wait(ag.at[p, far, pl.ds(AHALF, WA - AHALF)], r_fwd.at[p, 1])
            push(ag.at[p, far], ag.at[p, far], s_core.at[p], r_core.at[p], (e, mate))

        @pl.when(due(t, 4))
        def _():
            p = (t - 4 * STEP) // GAP
            left = block_of(c, x + NX - 1)
            right = block_of(c, x + 1)
            lo = pl.ds(0, AHALF)
            hi = pl.ds(AHALF, WA - AHALF)
            wait(ag.at[p, left], r_agx.at[p, 0])
            push(ag.at[p, left, lo], ag.at[p, left, lo], s_ag.at[p], r_fwd.at[p, 0], (e, xp))
            push(ag.at[p, left], ag.at[p, left], s_core.at[p], r_core.at[p], (e, mate))
            wait(ag.at[p, right], r_agx.at[p, 1])
            push(ag.at[p, right, hi], ag.at[p, right, hi], s_ag.at[p], r_fwd.at[p, 1], (e, xm))
            push(ag.at[p, right], ag.at[p, right], s_core.at[p], r_core.at[p], (e, mate))

        @pl.when(due(t, 3))
        def _():
            p = (t - 3 * STEP) // GAP
            wait(rb.at[p, 0], r_2b.at[p, 0])
            wait(rb.at[p, 1], r_2b.at[p, 1])
            own = rows_of(x)

            def total(lo, hi):
                return (
                    ss[p, own, lo:hi].astype(F32)
                    + rb[p, 0, :, lo:hi].astype(F32)
                    + rb[p, 1, :, lo:hi].astype(F32)
                )

            low = total(C_LOW, C_BACK).astype(BF)
            bl = total(C_BL, WP).astype(BF)
            left_half = lax.broadcasted_iota(jnp.int32, (BLK, LANE), 1) < 64
            low32 = low.astype(F32)
            low_g = jnp.where(left_half, low32, 0.0).astype(BF)
            low_u = jnp.where(left_half, 0.0, low32).astype(BF)
            gate = total(0, HID) + SCALE * dot(low_g, gb[...])
            up = total(HID, C_LOW) + SCALE * dot(low_u, gb[...])
            gh = total(C_BACK, C_BL) + SCALE * dot(bl[:, 0:64], da[...])
            sig = jax.nn.sigmoid(gate)
            act = gate * sig
            hidden = (act * up).astype(BF)
            gg = (gh * up * sig * (1.0 + gate * (1.0 - sig))).astype(BF)
            gup = (gh * act).astype(BF)
            hl = dot_t(hidden, da[...])
            lb = jnp.where(left_half, dot_t(gg, gb[...]), dot_t(gup, gb[...]))
            mine = block_of(c, x)
            ag[p, mine, 0:HID] = hidden
            ag[p, mine, HID : 2 * HID] = gg
            ag[p, mine, 2 * HID : A_LB] = gup
            ag[p, mine, A_LB:A_LOW] = lb.astype(BF)
            ag[p, mine, A_LOW:A_HB] = low
            ag[p, mine, A_HB:WA] = jnp.concatenate(
                [hl, bl[:, 0:64].astype(F32)], axis=1
            ).astype(BF)
            here = ag.at[p, mine]
            push(here, here, s_ag.at[p], r_agx.at[p, 0], (e, xp))
            push(here, here, s_ag.at[p], r_agx.at[p, 1], (e, xm))
            push(here, here, s_core.at[p], r_core.at[p], (e, mate))

        @pl.when(due(t, 2))
        def _():
            p = (t - 2 * STEP) // GAP
            right = rows_of(x + 1)
            left = rows_of(x + NX - 1)
            wait(ra.at[p, 0], r_2a.at[p, 0])
            ss[p, right, 0:HALF] = (
                ss[p, right, 0:HALF].astype(F32) + ra[p, 0].astype(F32)
            ).astype(BF)
            push(
                ss.at[p, right, first], rb.at[p, 0, rows16, first],
                s_rs.at[p], r_2b.at[p, 0], (e, xp),
            )
            wait(ra.at[p, 1], r_2a.at[p, 1])
            ss[p, left, HALF:WP] = (
                ss[p, left, HALF:WP].astype(F32) + ra[p, 1].astype(F32)
            ).astype(BF)
            push(
                ss.at[p, left, second], rb.at[p, 1, rows16, second],
                s_rs.at[p], r_2b.at[p, 1], (e, xm),
            )

        @pl.when(due(t, 1))
        def _():
            p = (t - 1 * STEP) // GAP
            wait(pr.at[p], r_pair.at[p])

            def add(i, carry):
                xx = (x + 2 + i) % NX
                mine = block_of(c, xx)
                at = rows_of(xx)
                ss[p, at, :] = (pt[p, mine, :].astype(F32) + pr[p, at, :].astype(F32)).astype(BF)

                @pl.when(i == 0)
                def _():
                    push(
                        ss.at[p, at, pl.ds(0, HALF)], ra.at[p, 0],
                        s_rs.at[p], r_2a.at[p, 0], (e, xp),
                    )
                    push(
                        ss.at[p, at, pl.ds(HALF, HALF)], ra.at[p, 1],
                        s_rs.at[p], r_2a.at[p, 1], (e, xm),
                    )

                return carry

            lax.fori_loop(0, NX, add, 0)
            push(
                ss.at[p, rows_of(x + 1), second], rb.at[p, 0, rows16, second],
                s_rs.at[p], r_2b.at[p, 0], (e, xp),
            )
            push(
                ss.at[p, rows_of(x + NX - 1), first], rb.at[p, 1, rows16, first],
                s_rs.at[p], r_2b.at[p, 1], (e, xm),
            )

        @pl.when(t == 0)
        def _():
            ring_wait(0)

        @pl.when(t == 1)
        def _():
            ring_wait(1)

        @pl.when(t == GAP)
        def _():
            ring_wait(2)

        @pl.when(t == 2 * GAP)
        def _():
            ring_wait(3)

        @pl.when(due(t, 0))
        def _():
            p = t // GAP
            for i in range(2):
                xv, gv = hot_rows(p, i)
                rs = slice(i * 64, (i + 1) * 64)
                xs[p, rs, :] = xv.astype(BF)
                gs[p, rs, :] = gv.astype(BF)

        @pl.when(t == GAP)
        def _():
            wait(nrecv.at[pl.ds(0, NZ), pl.ds(0, NY - 1)], r_n2)
            stage[...] = nrecv[...].reshape(COLS * 16, LANE).astype(F32)
            for r in range(2):
                for q in range(4):
                    cut = slice(q * LANE, (q + 1) * LANE)
                    rs = slice(r * COLS, (r + 1) * COLS)
                    xn = stage[pl.ds(r * 4 + q, COLS, stride=16), :]
                    gn = stage[pl.ds(8 + r * 4 + q, COLS, stride=16), :]
                    xs[1, rs, cut] = (xs[1, rs, cut].astype(F32) + xn).astype(BF)
                    gs[1, rs, cut] = (gs[1, rs, cut].astype(F32) + gn).astype(BF)

        @pl.when(due(t, 0))
        def _():
            partial(t // GAP)

        return carry

    lax.fori_loop(0, TICKS, tick, 0)

    xall = xs[...].reshape(PARTS * ROWS, DF)
    gall = gs[...].reshape(PARTS * ROWS, DF)

    def cols(lo, hi):
        return ag[:, :, lo:hi].reshape(PARTS * ROWS, hi - lo)

    gga_o[...] = SCALE * t_dot(cols(A_LB, A_LOW), xall).T
    hb = cols(A_HB, WA)
    gda_o[...] = SCALE * t_dot(hb, cols(0, HID))[64:128]
    gdb_o[...] = SCALE * t_dot(hb, gall)[0:64]

    for o in range(1, NZ):
        wait(hgot_a.at[o], r_ha.at[o])
    got = hret[0, 0, :, :, 0:CUT].astype(F32)
    for o in range(1, NZ):
        got = got + hgot_a[o].astype(F32)
    ysend[...] = got.astype(BF)
    for v in range(1, NY):
        to = (y + v) % NY
        push(ysend.at[to], ygot.at[v], s_w, r_w, (z * NY + to, d))
    for p in range(PARTS):
        wait(hgot_b.at[p, pl.ds(0, NY - 1)], r_hb.at[p])
        for i in range(2):
            o = offset(p, i)
            got = hret[p, i, y, :, CUT:DF].astype(F32)
            for v in range(1, NY):
                got = got + hgot_b[p, v, i].astype(F32)
            zsend[o] = got.astype(BF)
            if o > 0:
                push(zsend.at[o], zgot.at[o], s_v, r_v, (((z + o) % NZ) * NY + y, d))
    ygot[0] = ysend[y]
    zgot[0] = zsend[0]

    low = cols(A_LOW, A_HB)
    ggb_o[0:64, :] = SCALE * t_dot(low, cols(A_GB, A_GB + HID))[0:64]
    ggb_o[64:128, :] = SCALE * t_dot(low, cols(A_GB + HID, A_LB))[64:128]

    wait(cz.at[pl.ds(0, NZ - 1)], r_cz)
    total = jnp.sum(cz[...].astype(F32).reshape(NZ * 16, LANE), axis=0, keepdims=True)
    lane1 = lax.broadcasted_iota(jnp.int32, (1, LANE), 1)
    mine = jnp.sum(jnp.where(lane1 == e, total, 0.0)) * (1.0 / 16.0)
    held = (plc[0] == e) | (plc[1] == e) | (plc[2] == e) | (plc[3] == e)
    share = COLS // 4 * 8
    rows = jnp.where(hot == e, 0, mine.astype(jnp.int32)) + jnp.where(held, share, 0)
    rows_o[0] = rows
    blocks_o[0] = (rows + 127) // 128

    wait(nret.at[pl.ds(0, NZ - 1)], r_b2)
    stage[...] = nret[...].reshape(COLS * 16, LANE).astype(F32)
    ordinary = []
    for q in range(4):
        mix = jnp.zeros((TOK, LANE), F32)
        gt = jnp.zeros((TOK, LANE), F32)
        for r in range(2):
            rows_out = stage[pl.ds(r * 4 + q, COLS, stride=16), :].astype(BF)
            rows_dx = stage[pl.ds(8 + r * 4 + q, COLS, stride=16), :].astype(BF)
            mix = mix + t_dot(route[2 + 2 * r], rows_out) + t_dot(route[3 + 2 * r], rows_out)
            gt = gt + t_dot(route[r], rows_dx)
        ordinary.append((mix, gt))

    wait(ygot.at[pl.ds(1, NY - 1)], r_w)
    wait(zgot.at[pl.ds(1, NZ - 1)], r_v)
    for h, got in enumerate((ygot, zgot)):
        back = got[0].astype(F32)
        for o in range(1, NY):
            back = back + got[o].astype(F32)
        for q in range(2):
            cut = slice(q * LANE, (q + 1) * LANE)
            mix, gt = ordinary[2 * h + q]
            for r in range(8):
                mix = mix + hroute[1][:, r : r + 1] * back[r : r + 1, cut]
                gt = gt + hroute[0][:, r : r + 1] * back[8 + r : 9 + r, cut]
            at = slice((2 * h + q) * LANE, (2 * h + q + 1) * LANE)
            mixed_o[:, at] = mix.astype(BF)
            gtok_o[:, at] = gt.astype(BF)

    wait(nsend.at[pl.ds(0, NZ - 1)], s_n)
    wait(nmid.at[pl.ds(0, NZ), pl.ds(0, NY - 1)], s_n2)
    wait(nback.at[pl.ds(0, NZ), pl.ds(0, NY - 1)], s_b)
    wait(nhalf.at[pl.ds(0, NZ - 1)], s_b2)
    wait(hg.at[z, pl.ds(0, NY - 1)], s_y)
    for h in range(2):
        for s in range(4):
            wait(plane_half(0, h), s_zp.at[s, h])
        for s in range(3):
            wait(plane_half(0, h), s_zm.at[s, h])
    wait(cy.at[pl.ds(0, NY - 1)], s_cy)
    wait(cz.at[pl.ds(0, NZ - 1)], s_cz)
    wait(hgot_a.at[pl.ds(1, NZ - 1)], s_ha)
    wait(hgot_b.at[pl.ds(0, PARTS), pl.ds(0, NY - 1)], s_hb)
    wait(ysend.at[pl.ds(0, NY - 1)], s_w)
    wait(zsend.at[pl.ds(0, NZ - 1)], s_v)
    for p in range(PARTS):
        wait(pt.at[p, pl.ds(0, 64)], s_pair.at[p])
        wait(ss.at[p, pl.ds(0, 48)], s_rs.at[p])
        wait(ag.at[p, pl.ds(0, 48)], s_ag.at[p])
        wait(ag.at[p, pl.ds(0, 64)], s_core.at[p])


def copy_kernel(*refs):
    n = len(refs) // 2
    for i in range(n):
        refs[n + i][...] = refs[i][...]


def hand_over(arrays):
    vmem = pl.BlockSpec(memory_space=pltpu.VMEM)
    return pl.pallas_call(
        copy_kernel,
        out_shape=tuple(jax.ShapeDtypeStruct(a.shape, a.dtype) for a in arrays),
        in_specs=[vmem] * len(arrays),
        out_specs=tuple([vmem] * len(arrays)),
    )(*arrays)


def per_device(
    tokens, expert_ids, route_weight, placement, gate_up_base, down_base, gate_up_a, gate_up_b,
    down_a, down_b, grad_mixed,
):
    vmem = pl.BlockSpec(memory_space=pltpu.VMEM)
    smem = pl.BlockSpec(memory_space=pltpu.SMEM)
    hbm = pl.BlockSpec(memory_space=pl.ANY)
    dma = pltpu.SemaphoreType.DMA
    out = pl.pallas_call(
        kernel,
        out_shape=(
            jax.ShapeDtypeStruct((TOK, DF), BF),
            jax.ShapeDtypeStruct((TOK, DF), BF),
            jax.ShapeDtypeStruct((DF, 128), F32),
            jax.ShapeDtypeStruct((128, HID), F32),
            jax.ShapeDtypeStruct((64, HID), F32),
            jax.ShapeDtypeStruct((64, DF), F32),
            jax.ShapeDtypeStruct((1,), jnp.int32),
            jax.ShapeDtypeStruct((1,), jnp.int32),
        ),
        in_specs=[vmem] * 4 + [smem] + [hbm] * 6,
        out_specs=[vmem] * 6 + [smem] * 2,
        scratch_shapes=[
            pltpu.VMEM((DF, 2 * HID), BF),
            pltpu.VMEM((HID, DF), BF),
            pltpu.VMEM((DF, 128), BF),
            pltpu.VMEM((128, HID), BF),
            pltpu.VMEM((64, HID), BF),
            pltpu.VMEM((128, DF), BF),
            dma((6,)),
            pltpu.VMEM((6, COLS, TOK), BF),
            pltpu.VMEM((2, TOK, 8), F32),
            pltpu.VMEM((COLS * 16, LANE), F32),
            pltpu.VMEM((NZ, NY, 16, LANE), BF),
            pltpu.VMEM((NZ, NY, 16, LANE), BF),
            pltpu.VMEM((NZ, NY, 16, LANE), BF),
            pltpu.VMEM((NZ, NY, 16, LANE), BF),
            pltpu.VMEM((NZ, NY, 16, LANE), BF),
            pltpu.VMEM((NZ, NY, 16, LANE), BF),
            pltpu.VMEM((NZ, NY, 16, DF), BF),
            pltpu.VMEM((PARTS, ROWS, DF), BF),
            pltpu.VMEM((PARTS, ROWS, DF), BF),
            pltpu.VMEM((PARTS, ROWS, WP), BF),
            pltpu.VMEM((PARTS, 64, WP), BF),
            pltpu.VMEM((PARTS, 64, WP), BF),
            pltpu.VMEM((PARTS, 2, BLK, HALF), BF),
            pltpu.VMEM((PARTS, 2, BLK, WP), BF),
            pltpu.VMEM((PARTS, ROWS, WA), BF),
            pltpu.VMEM((PARTS, 2, NY, 16, DF), BF),
            pltpu.VMEM((NZ, NY, 16, CUT), BF),
            pltpu.VMEM((PARTS, NY, 2, 16, DF - CUT), BF),
            pltpu.VMEM((NY, 16, CUT), BF),
            pltpu.VMEM((NY, 16, CUT), BF),
            pltpu.VMEM((NZ, 16, DF - CUT), BF),
            pltpu.VMEM((NZ, 16, DF - CUT), BF),
            pltpu.VMEM((NY, 16, LANE), BF),
            pltpu.VMEM((NZ, 16, LANE), BF),
            dma, dma, dma, dma, dma, dma, dma, dma, dma, dma,
            dma((4, 2)), dma((4, 2)), dma((3, 2)), dma((3, 2)),
            dma, dma, dma, dma,
            dma, dma((NZ,)), dma, dma((PARTS,)), dma, dma, dma, dma,
            dma((PARTS,)), dma((PARTS,)),
            dma((PARTS,)), dma((PARTS, 2)), dma((PARTS, 2)),
            dma((PARTS,)), dma((PARTS, 2)), dma((PARTS, 2)),
            dma((PARTS,)), dma((PARTS,)),
        ],
        compiler_params=pltpu.CompilerParams(
            collective_id=0, has_side_effects=True, vmem_limit_bytes=56 * 1024 * 1024
        ),
    )(
        tokens, expert_ids.T, route_weight.T, grad_mixed, placement, gate_up_base[0], down_base[0],
        gate_up_a[0], gate_up_b[0], down_a[0].T, down_b[0],
    )
    mixed, gtok, gga, ggb, gda, gdb = hand_over(out[:6])
    return mixed, gtok, gga[None], ggb[None], gda.T[None], gdb[None], out[6], out[7]


def solution(mesh):
    return jax.shard_map(
        per_device,
        mesh=mesh,
        in_specs=(
            P("expert", "dp"),
            P("expert", None),
            P("expert", None),
            P(),
            P("expert", "dp", None),
            P("expert", None, "dp"),
            P("expert", "dp", None),
            P("expert", None, None),
            P("expert", None, None),
            P("expert", None, "dp"),
            P("expert", "dp"),
        ),
        out_specs=(
            P("expert", "dp"),
            P("expert", "dp"),
            P("expert", "dp", None),
            P("expert", None, None),
            P("expert", None, None),
            P("expert", None, "dp"),
            P("expert"),
            P("expert"),
        ),
        check_vma=False,
    )
```

```python
import jax
import jax.numpy as jnp
from jax import lax
from jax.experimental import pallas as pl
from jax.experimental.pallas import tpu as pltpu
from jax.sharding import PartitionSpec as P

SCALE = 0.25
BF = jnp.bfloat16
F32 = jnp.float32
NY, NZ, NX = 8, 8, 4
COLS = NY * NZ
TOK = 16
DF = 512
HID = 1024
PARTS = 4
ROWS = 128
BLK = 16
LANE = 128
C_LOW, C_BACK, C_BL, WP = 2048, 2176, 3200, 3328
HALF = 1664
A_GB, A_LB, A_LOW, A_HB, WA = 1024, 3072, 3200, 3328, 3456
AHALF = 1792
CUT = 256
GAP, STEP = 1, 1
TICKS = GAP * (PARTS - 1) + 6 * STEP + 1


def dot(a, b):
    return jnp.dot(a, b, preferred_element_type=F32)


def dot_t(a, b):
    return lax.dot_general(a, b, (((1,), (1,)), ((), ())), preferred_element_type=F32)


def t_dot(a, b):
    return lax.dot_general(a, b, (((0,), (0,)), ((), ())), preferred_element_type=F32)


def kernel(
    tok, ids, rw, grad, plc, gu_h, dn_h, ga_h, gb_h, da_h, db_h,
    mixed_o, gtok_o, gga_o, ggb_o, gda_o, gdb_o, rows_o, blocks_o,
    gu, dn, ga, gb, da, db, wsem,
    route, hroute, stage, nsend, nmid, nrecv, nback, nhalf, nret, hg, xs, gs, pt, pr, ss, ra, rb, ag,
    hret, hgot_a, hgot_b, ysend, ygot, zsend, zgot,
    cy, cz, s_n, r_n, s_n2, r_n2, s_b, r_b, s_b2, r_b2, s_y, r_y, s_zp, r_zp, s_zm, r_zm,
    s_cy, r_cy, s_cz, r_cz, s_ha, r_ha, s_hb, r_hb, s_w, r_w, s_v, r_v,
    s_pair, r_pair, s_rs, r_2a, r_2b, s_ag, r_agx, r_fwd, s_core, r_core,
):
    e = lax.axis_index("expert")
    d = lax.axis_index("dp")
    z, y = e // NY, e % NY
    x, c = d // 2, d % 2

    def push(src, dst, ssem, rsem, dev):
        pltpu.make_async_remote_copy(
            src_ref=src, dst_ref=dst, send_sem=ssem, recv_sem=rsem, device_id=dev,
            device_id_type=pl.DeviceIdType.MESH,
        ).start()

    def wait(ref, sem):
        pltpu.make_async_copy(ref, ref, sem).wait()

    xp = ((x + 1) % NX) * 2 + c
    xm = ((x + NX - 1) % NX) * 2 + c
    mate = x * 2 + (1 - c)

    barrier = pltpu.get_barrier_semaphore()

    for o in range(1, NY):
        for peer in (z * NY + (y + o) % NY, ((z + o) % NZ) * NY + y):
            pl.semaphore_signal(
                barrier, inc=1, device_id=(peer, d), device_id_type=pl.DeviceIdType.MESH
            )
    for peer in (xp, xm, mate):
        pl.semaphore_signal(
            barrier, inc=1, device_id=(e, peer), device_id_type=pl.DeviceIdType.MESH
        )

    loads = [
        pltpu.make_async_copy(src, dst, wsem.at[i])
        for i, (src, dst) in enumerate(
            ((gu_h, gu), (dn_h, dn), (ga_h, ga), (gb_h, gb), (da_h, da), (db_h, db.at[0:64]))
        )
    ]
    for load in loads:
        load.start()

    db[64:128, :] = jnp.zeros((64, DF), BF)

    hot = plc[0]
    is_hot = (hot == e).astype(F32)
    row_i = lax.broadcasted_iota(jnp.int32, (TOK, TOK), 0)
    col_i = lax.broadcasted_iota(jnp.int32, (TOK, TOK), 1)
    before = jnp.where(row_i < col_i, 1.0, 0.0).astype(BF)

    def membership(expert):
        member = jnp.zeros(expert.shape, F32)
        weight = jnp.zeros(expert.shape, F32)
        for k in range(ids.shape[0]):
            same = ids[k : k + 1, :] == expert
            member = member + jnp.where(same, 1.0, 0.0)
            weight = weight + jnp.where(same, rw[k : k + 1, :], 0.0)
        return member, weight, dot(member.astype(BF), before)

    expert = lax.broadcasted_iota(jnp.int32, (LANE, TOK), 0)
    member, weight, rank = membership(expert)
    hot_row = jnp.where(expert == hot, 1.0, 0.0)
    tokens = tok[...]
    grads = grad[...]
    hm = jnp.sum(member * hot_row, axis=0, keepdims=True)
    hw = jnp.sum(weight * hot_row, axis=0, keepdims=True)
    hr = jnp.sum(rank * hot_row, axis=0, keepdims=True)
    place = lax.broadcasted_iota(jnp.int32, (8, TOK), 0).astype(F32)
    hpick = jnp.where(place == hr, hm, 0.0)
    hpw = hpick * hw
    hroute[0] = hpick.T
    hroute[1] = hpw.T
    hx = dot(hpick.astype(BF), tokens)
    hgr = dot(hpick.astype(BF), grads) * jnp.sum(hpw, axis=1, keepdims=True)
    hg[z, y] = jnp.concatenate([hx, hgr], axis=0).astype(BF)
    cy[0] = dot_t(jnp.ones((16, TOK), BF), member.astype(BF)).astype(BF)

    pl.semaphore_wait(barrier, NY - 1 + NZ - 1 + 3)

    lo, hi = pl.ds(0, CUT), pl.ds(CUT, DF - CUT)
    for o in range(1, NY):
        push(hg.at[z, y], hg.at[z, y], s_y, r_y, (z * NY + (y + o) % NY, d))
    def keep(at, value):
        head = value.astype(BF)
        route[at] = head
        route[at + 1] = (value - head.astype(F32)).astype(BF)

    away = lax.broadcasted_iota(jnp.int32, (COLS, TOK), 0)
    there = ((z + (away >> 3)) & (NZ - 1)) * NY + ((y + (away & 7)) & (NY - 1))
    near, near_w, near_rank = membership(there)
    cold = jnp.where(there == hot, 0.0, near)
    for r in range(2):
        pick = jnp.where(near_rank == r, cold, 0.0)
        pw = pick * near_w
        route[r] = pick.astype(BF)
        keep(2 + 2 * r, pw)
        xr = dot(pick.astype(BF), tokens)
        gr = dot(pick.astype(BF), grads) * jnp.sum(pw, axis=1, keepdims=True)
        for q in range(4):
            cut = slice(q * LANE, (q + 1) * LANE)
            stage[pl.ds(r * 4 + q, COLS, stride=16), :] = xr[:, cut]
            stage[pl.ds(8 + r * 4 + q, COLS, stride=16), :] = gr[:, cut]
    nsend[...] = stage[...].astype(BF).reshape(NZ, NY, 16, LANE)
    for o in range(1, NZ):
        push(nsend.at[o], nmid.at[o], s_n, r_n, (((z + o) % NZ) * NY + y, d))
    nmid[0] = nsend[0]

    zp = ((z + 1) % NZ) * NY + y
    zm = ((z + NZ - 1) % NZ) * NY + y
    rows16 = pl.ds(0, 16)

    def plane_half(at, h):
        return hg.at[at % NZ, pl.ds(0, NY), rows16, (lo, hi)[h]]

    def ring_send(s, h):
        up = plane_half(z + NZ - s, h)
        push(up, up, s_zp.at[s, h], r_zp.at[s, h], (zp, d))
        if s < 3:
            down = plane_half(z + s, h)
            push(down, down, s_zm.at[s, h], r_zm.at[s, h], (zm, d))

    def ring_wait(s):
        for h in range(2):
            wait(plane_half(0, h), r_zp.at[s, h])
            if s < 3:
                wait(plane_half(0, h), r_zm.at[s, h])
                ring_send(s + 1, h)

    wait(hg.at[z, pl.ds(0, NY - 1)], r_y)
    ring_send(0, 0)
    ring_send(0, 1)

    wait(nmid.at[pl.ds(0, NZ - 1)], r_n)
    for o in range(1, NY):
        push(
            nmid.at[pl.ds(0, NZ), o], nrecv.at[pl.ds(0, NZ), o], s_n2, r_n2,
            (z * NY + (y + o) % NY, d),
        )
    nrecv[:, 0] = nmid[:, 0]
    for o in range(1, NY):
        push(cy.at[0], cy.at[o], s_cy, r_cy, (z * NY + (y + o) % NY, d))
    for load in loads:
        load.wait()

    def offset(p, i):
        first = (p + 2) * ((p + 2) // 3) - 3 * (p // 3)
        return first if i == 0 else (9 - first) % NZ

    def hot_rows(p, i):
        v = hg[(z + offset(p, i)) % NZ].astype(F32) * is_hot
        return v[:, 0:8, :].reshape(64, DF), v[:, 8:16, :].reshape(64, DF)

    def partial(p):
        xv = xs[p]
        gv = gs[p]

        def one(n, carry):
            at = pl.ds(pl.multiple_of(n * 512, 512), 512)
            pt[p, :, at] = dot(xv, gu[:, at]).astype(BF)
            return carry

        lax.fori_loop(0, 4, one, 0)
        pt[p, :, C_LOW:C_BACK] = dot(xv, ga[...]).astype(BF)
        for n in range(2):
            pt[p, :, C_BACK + n * 512 : C_BACK + (n + 1) * 512] = dot_t(
                gv, dn[n * 512 : (n + 1) * 512, :]
            ).astype(BF)
        pt[p, :, C_BL:WP] = dot_t(gv, db[...]).astype(BF)
        push(
            pt.at[p, pl.ds(pl.multiple_of((1 - c) * 64, 64), 64)], pr.at[p],
            s_pair.at[p], r_pair.at[p], (e, mate),
        )

    def rows_of(xx):
        return pl.ds(pl.multiple_of((xx % NX) * BLK, BLK), BLK)

    def block_of(core, xx):
        return pl.ds(pl.multiple_of((core * NX + xx % NX) * BLK, BLK), BLK)

    def due(t, stage):
        since = t - stage * STEP
        return (since >= 0) & (since < GAP * PARTS) & ((since + 6 * STEP * GAP) % GAP == 0)

    first, second = pl.ds(0, HALF), pl.ds(HALF, HALF)

    def tick(t, carry):
        @pl.when(due(t, 6))
        def _():
            p = (t - 6 * STEP) // GAP
            wait(ag.at[p, pl.ds(0, 64)], r_core.at[p])
            hid = ag[p, :, 0:HID]
            hb = ag[p, :, A_HB:WA]
            out = dot(hid, dn[...]) + SCALE * dot(hb, db[...])
            both = ag[p, :, A_GB:A_LB]
            lb = ag[p, :, A_LB:A_LOW]
            dx = dot_t(both, gu[...]) + SCALE * dot_t(lb, ga[...])

            for i in range(2):
                o = offset(p, i)
                rs = slice(i * 64, (i + 1) * 64)
                block = jnp.concatenate(
                    [out[rs].reshape(NY, 8, DF), dx[rs].reshape(NY, 8, DF)], axis=1
                )
                hret[p, i] = (block * is_hot).astype(BF)

                @pl.when(o > 0)
                def _():
                    push(
                        hret.at[p, i, pl.ds(0, NY), rows16, lo], hgot_a.at[o], s_ha, r_ha.at[o],
                        (((z + o) % NZ) * NY + y, d),
                    )

            for v in range(1, NY):
                to = (y + v) % NY
                push(
                    hret.at[p, pl.ds(0, 2), to, rows16, hi], hgot_b.at[p, v], s_hb, r_hb.at[p],
                    (z * NY + to, d),
                )

            @pl.when(p == 1)
            def _():
                for r in range(2):
                    for q in range(4):
                        cut = slice(q * LANE, (q + 1) * LANE)
                        rs = slice(r * COLS, (r + 1) * COLS)
                        stage[pl.ds(r * 4 + q, COLS, stride=16), :] = out[rs, cut]
                        stage[pl.ds(8 + r * 4 + q, COLS, stride=16), :] = dx[rs, cut]
                nback[...] = stage[...].astype(BF).reshape(NZ, NY, 16, LANE)
                for v in range(1, NY):
                    push(
                        nback.at[pl.ds(0, NZ), v], nhalf.at[pl.ds(0, NZ), v], s_b, r_b,
                        (z * NY + (y + NY - v) % NY, d),
                    )
                nhalf[:, 0] = nback[:, 0]

        @pl.when(t == GAP + 6 * STEP + 2)
        def _():
            wait(nhalf.at[pl.ds(0, NZ), pl.ds(0, NY - 1)], r_b)
            for o in range(1, NZ):
                push(nhalf.at[o], nret.at[o], s_b2, r_b2, (((z + NZ - o) % NZ) * NY + y, d))
            nret[0] = nhalf[0]

        @pl.when(due(t, 5))
        def _():
            p = (t - 5 * STEP) // GAP
            far = block_of(c, x + 2)
            wait(ag.at[p, far, pl.ds(0, AHALF)], r_fwd.at[p, 0])
            wait(ag.at[p, far, pl.ds(AHALF, WA - AHALF)], r_fwd.at[p, 1])
            push(ag.at[p, far], ag.at[p, far], s_core.at[p], r_core.at[p], (e, mate))

        @pl.when(due(t, 4))
        def _():
            p = (t - 4 * STEP) // GAP
            left = block_of(c, x + NX - 1)
            right = block_of(c, x + 1)
            lo = pl.ds(0, AHALF)
            hi = pl.ds(AHALF, WA - AHALF)
            wait(ag.at[p, left], r_agx.at[p, 0])
            push(ag.at[p, left, lo], ag.at[p, left, lo], s_ag.at[p], r_fwd.at[p, 0], (e, xp))
            push(ag.at[p, left], ag.at[p, left], s_core.at[p], r_core.at[p], (e, mate))
            wait(ag.at[p, right], r_agx.at[p, 1])
            push(ag.at[p, right, hi], ag.at[p, right, hi], s_ag.at[p], r_fwd.at[p, 1], (e, xm))
            push(ag.at[p, right], ag.at[p, right], s_core.at[p], r_core.at[p], (e, mate))

        @pl.when(due(t, 3))
        def _():
            p = (t - 3 * STEP) // GAP
            wait(rb.at[p, 0], r_2b.at[p, 0])
            wait(rb.at[p, 1], r_2b.at[p, 1])
            own = rows_of(x)

            def total(lo, hi):
                return (
                    ss[p, own, lo:hi].astype(F32)
                    + rb[p, 0, :, lo:hi].astype(F32)
                    + rb[p, 1, :, lo:hi].astype(F32)
                )

            low = total(C_LOW, C_BACK).astype(BF)
            bl = total(C_BL, WP).astype(BF)
            left_half = lax.broadcasted_iota(jnp.int32, (BLK, LANE), 1) < 64
            low32 = low.astype(F32)
            low_g = jnp.where(left_half, low32, 0.0).astype(BF)
            low_u = jnp.where(left_half, 0.0, low32).astype(BF)
            gate = total(0, HID) + SCALE * dot(low_g, gb[...])
            up = total(HID, C_LOW) + SCALE * dot(low_u, gb[...])
            gh = total(C_BACK, C_BL) + SCALE * dot(bl[:, 0:64], da[...])
            sig = jax.nn.sigmoid(gate)
            act = gate * sig
            hidden = (act * up).astype(BF)
            gg = (gh * up * sig * (1.0 + gate * (1.0 - sig))).astype(BF)
            gup = (gh * act).astype(BF)
            hl = dot_t(hidden, da[...])
            lb = jnp.where(left_half, dot_t(gg, gb[...]), dot_t(gup, gb[...]))
            mine = block_of(c, x)
            ag[p, mine, 0:HID] = hidden
            ag[p, mine, HID : 2 * HID] = gg
            ag[p, mine, 2 * HID : A_LB] = gup
            ag[p, mine, A_LB:A_LOW] = lb.astype(BF)
            ag[p, mine, A_LOW:A_HB] = low
            ag[p, mine, A_HB:WA] = jnp.concatenate(
                [hl, bl[:, 0:64].astype(F32)], axis=1
            ).astype(BF)
            here = ag.at[p, mine]
            push(here, here, s_ag.at[p], r_agx.at[p, 0], (e, xp))
            push(here, here, s_ag.at[p], r_agx.at[p, 1], (e, xm))
            push(here, here, s_core.at[p], r_core.at[p], (e, mate))

        @pl.when(due(t, 2))
        def _():
            p = (t - 2 * STEP) // GAP
            right = rows_of(x + 1)
            left = rows_of(x + NX - 1)
            wait(ra.at[p, 0], r_2a.at[p, 0])
            ss[p, right, 0:HALF] = (
                ss[p, right, 0:HALF].astype(F32) + ra[p, 0].astype(F32)
            ).astype(BF)
            push(
                ss.at[p, right, first], rb.at[p, 0, rows16, first],
                s_rs.at[p], r_2b.at[p, 0], (e, xp),
            )
            wait(ra.at[p, 1], r_2a.at[p, 1])
            ss[p, left, HALF:WP] = (
                ss[p, left, HALF:WP].astype(F32) + ra[p, 1].astype(F32)
            ).astype(BF)
            push(
                ss.at[p, left, second], rb.at[p, 1, rows16, second],
                s_rs.at[p], r_2b.at[p, 1], (e, xm),
            )

        @pl.when(due(t, 1))
        def _():
            p = (t - 1 * STEP) // GAP
            wait(pr.at[p], r_pair.at[p])

            def add(i, carry):
                xx = (x + 2 + i) % NX
                mine = block_of(c, xx)
                at = rows_of(xx)
                ss[p, at, :] = (pt[p, mine, :].astype(F32) + pr[p, at, :].astype(F32)).astype(BF)

                @pl.when(i == 0)
                def _():
                    push(
                        ss.at[p, at, pl.ds(0, HALF)], ra.at[p, 0],
                        s_rs.at[p], r_2a.at[p, 0], (e, xp),
                    )
                    push(
                        ss.at[p, at, pl.ds(HALF, HALF)], ra.at[p, 1],
                        s_rs.at[p], r_2a.at[p, 1], (e, xm),
                    )

                return carry

            lax.fori_loop(0, NX, add, 0)
            push(
                ss.at[p, rows_of(x + 1), second], rb.at[p, 0, rows16, second],
                s_rs.at[p], r_2b.at[p, 0], (e, xp),
            )
            push(
                ss.at[p, rows_of(x + NX - 1), first], rb.at[p, 1, rows16, first],
                s_rs.at[p], r_2b.at[p, 1], (e, xm),
            )

        @pl.when(t == 0)
        def _():
            ring_wait(0)

        @pl.when(t == 1)
        def _():
            ring_wait(1)

        @pl.when(t == GAP)
        def _():
            ring_wait(2)

        @pl.when(t == 2 * GAP)
        def _():
            ring_wait(3)

        @pl.when(due(t, 0))
        def _():
            p = t // GAP
            for i in range(2):
                xv, gv = hot_rows(p, i)
                rs = slice(i * 64, (i + 1) * 64)
                xs[p, rs, :] = xv.astype(BF)
                gs[p, rs, :] = gv.astype(BF)

        @pl.when(t == GAP)
        def _():
            wait(nrecv.at[pl.ds(0, NZ), pl.ds(0, NY - 1)], r_n2)
            stage[...] = nrecv[...].reshape(COLS * 16, LANE).astype(F32)
            for r in range(2):
                for q in range(4):
                    cut = slice(q * LANE, (q + 1) * LANE)
                    rs = slice(r * COLS, (r + 1) * COLS)
                    xn = stage[pl.ds(r * 4 + q, COLS, stride=16), :]
                    gn = stage[pl.ds(8 + r * 4 + q, COLS, stride=16), :]
                    xs[1, rs, cut] = (xs[1, rs, cut].astype(F32) + xn).astype(BF)
                    gs[1, rs, cut] = (gs[1, rs, cut].astype(F32) + gn).astype(BF)

        @pl.when(due(t, 0))
        def _():
            partial(t // GAP)

        @pl.when(t == 4)
        def _():
            wait(cy.at[pl.ds(0, NY - 1)], r_cy)
            count = cy[0].astype(F32)
            for o in range(1, NY):
                count = count + cy[o].astype(F32)
            cz[0] = count.astype(BF)
            for o in range(1, NZ):
                push(cz.at[0], cz.at[o], s_cz, r_cz, (((z + o) % NZ) * NY + y, d))

        return carry

    lax.fori_loop(0, TICKS, tick, 0)

    def along_y(p):
        wait(hgot_b.at[p, pl.ds(0, NY - 1)], r_hb.at[p])
        for i in range(2):
            o = offset(p, i)
            got = hret[p, i, y, :, CUT:DF].astype(F32)
            for v in range(1, NY):
                got = got + hgot_b[p, v, i].astype(F32)
            zsend[o] = got.astype(BF)
            if o > 0:
                push(zsend.at[o], zgot.at[o], s_v, r_v, (((z + o) % NZ) * NY + y, d))

    for p in range(PARTS - 1):
        along_y(p)

    xall = xs[...].reshape(PARTS * ROWS, DF)
    gall = gs[...].reshape(PARTS * ROWS, DF)

    def cols(lo, hi):
        return ag[:, :, lo:hi].reshape(PARTS * ROWS, hi - lo)

    gga_o[...] = SCALE * t_dot(cols(A_LB, A_LOW), xall).T
    hb = cols(A_HB, WA)
    gda_o[...] = SCALE * t_dot(hb, cols(0, HID))[64:128]
    gdb_o[...] = SCALE * t_dot(hb, gall)[0:64]

    order = [offset(p, i) for p in range(PARTS) for i in range(2)]
    got = hret[0, 0, :, :, 0:CUT].astype(F32)
    for o in order[1:]:
        wait(hgot_a.at[o], r_ha.at[o])
        got = got + hgot_a[o].astype(F32)
    ysend[...] = got.astype(BF)
    for v in range(1, NY):
        to = (y + v) % NY
        push(ysend.at[to], ygot.at[v], s_w, r_w, (z * NY + to, d))
    along_y(PARTS - 1)
    ygot[0] = ysend[y]
    zgot[0] = zsend[0]

    low = cols(A_LOW, A_HB)
    ggb_o[0:64, :] = SCALE * t_dot(low, cols(A_GB, A_GB + HID))[0:64]
    ggb_o[64:128, :] = SCALE * t_dot(low, cols(A_GB + HID, A_LB))[64:128]

    wait(cz.at[pl.ds(0, NZ - 1)], r_cz)
    total = jnp.sum(cz[...].astype(F32).reshape(NZ * 16, LANE), axis=0, keepdims=True)
    lane1 = lax.broadcasted_iota(jnp.int32, (1, LANE), 1)
    mine = jnp.sum(jnp.where(lane1 == e, total, 0.0)) * (1.0 / 16.0)
    held = (plc[0] == e) | (plc[1] == e) | (plc[2] == e) | (plc[3] == e)
    share = COLS // 4 * 8
    rows = jnp.where(hot == e, 0, mine.astype(jnp.int32)) + jnp.where(held, share, 0)
    rows_o[0] = rows
    blocks_o[0] = (rows + 127) // 128

    wait(nret.at[pl.ds(0, NZ - 1)], r_b2)
    stage[...] = nret[...].reshape(COLS * 16, LANE).astype(F32)
    ordinary = []
    for q in range(4):
        mix = jnp.zeros((TOK, LANE), F32)
        gt = jnp.zeros((TOK, LANE), F32)
        for r in range(2):
            rows_out = stage[pl.ds(r * 4 + q, COLS, stride=16), :].astype(BF)
            rows_dx = stage[pl.ds(8 + r * 4 + q, COLS, stride=16), :].astype(BF)
            mix = mix + t_dot(route[2 + 2 * r], rows_out) + t_dot(route[3 + 2 * r], rows_out)
            gt = gt + t_dot(route[r], rows_dx)
        ordinary.append((mix, gt))

    wait(ygot.at[pl.ds(1, NY - 1)], r_w)
    wait(zgot.at[pl.ds(1, NZ - 1)], r_v)
    for h, got in enumerate((ygot, zgot)):
        back = got[0].astype(F32)
        for o in range(1, NY):
            back = back + got[o].astype(F32)
        for q in range(2):
            cut = slice(q * LANE, (q + 1) * LANE)
            mix, gt = ordinary[2 * h + q]
            for r in range(8):
                mix = mix + hroute[1][:, r : r + 1] * back[r : r + 1, cut]
                gt = gt + hroute[0][:, r : r + 1] * back[8 + r : 9 + r, cut]
            at = slice((2 * h + q) * LANE, (2 * h + q + 1) * LANE)
            mixed_o[:, at] = mix.astype(BF)
            gtok_o[:, at] = gt.astype(BF)

    wait(nsend.at[pl.ds(0, NZ - 1)], s_n)
    wait(nmid.at[pl.ds(0, NZ), pl.ds(0, NY - 1)], s_n2)
    wait(nback.at[pl.ds(0, NZ), pl.ds(0, NY - 1)], s_b)
    wait(nhalf.at[pl.ds(0, NZ - 1)], s_b2)
    wait(hg.at[z, pl.ds(0, NY - 1)], s_y)
    for h in range(2):
        for s in range(4):
            wait(plane_half(0, h), s_zp.at[s, h])
        for s in range(3):
            wait(plane_half(0, h), s_zm.at[s, h])
    wait(cy.at[pl.ds(0, NY - 1)], s_cy)
    wait(cz.at[pl.ds(0, NZ - 1)], s_cz)
    wait(hgot_a.at[pl.ds(1, NZ - 1)], s_ha)
    wait(hgot_b.at[pl.ds(0, PARTS), pl.ds(0, NY - 1)], s_hb)
    wait(ysend.at[pl.ds(0, NY - 1)], s_w)
    wait(zsend.at[pl.ds(0, NZ - 1)], s_v)
    for p in range(PARTS):
        wait(pt.at[p, pl.ds(0, 64)], s_pair.at[p])
        wait(ss.at[p, pl.ds(0, 48)], s_rs.at[p])
        wait(ag.at[p, pl.ds(0, 48)], s_ag.at[p])
        wait(ag.at[p, pl.ds(0, 64)], s_core.at[p])


def copy_kernel(*refs):
    n = len(refs) // 2
    for i in range(n):
        refs[n + i][...] = refs[i][...]


def hand_over(arrays):
    vmem = pl.BlockSpec(memory_space=pltpu.VMEM)
    return pl.pallas_call(
        copy_kernel,
        out_shape=tuple(jax.ShapeDtypeStruct(a.shape, a.dtype) for a in arrays),
        in_specs=[vmem] * len(arrays),
        out_specs=tuple([vmem] * len(arrays)),
    )(*arrays)


def per_device(
    tokens, expert_ids, route_weight, placement, gate_up_base, down_base, gate_up_a, gate_up_b,
    down_a, down_b, grad_mixed,
):
    vmem = pl.BlockSpec(memory_space=pltpu.VMEM)
    smem = pl.BlockSpec(memory_space=pltpu.SMEM)
    hbm = pl.BlockSpec(memory_space=pl.ANY)
    dma = pltpu.SemaphoreType.DMA
    out = pl.pallas_call(
        kernel,
        out_shape=(
            jax.ShapeDtypeStruct((TOK, DF), BF),
            jax.ShapeDtypeStruct((TOK, DF), BF),
            jax.ShapeDtypeStruct((DF, 128), F32),
            jax.ShapeDtypeStruct((128, HID), F32),
            jax.ShapeDtypeStruct((64, HID), F32),
            jax.ShapeDtypeStruct((64, DF), F32),
            jax.ShapeDtypeStruct((1,), jnp.int32),
            jax.ShapeDtypeStruct((1,), jnp.int32),
        ),
        in_specs=[vmem] * 4 + [smem] + [hbm] * 6,
        out_specs=[vmem] * 6 + [smem] * 2,
        scratch_shapes=[
            pltpu.VMEM((DF, 2 * HID), BF),
            pltpu.VMEM((HID, DF), BF),
            pltpu.VMEM((DF, 128), BF),
            pltpu.VMEM((128, HID), BF),
            pltpu.VMEM((64, HID), BF),
            pltpu.VMEM((128, DF), BF),
            dma((6,)),
            pltpu.VMEM((6, COLS, TOK), BF),
            pltpu.VMEM((2, TOK, 8), F32),
            pltpu.VMEM((COLS * 16, LANE), F32),
            pltpu.VMEM((NZ, NY, 16, LANE), BF),
            pltpu.VMEM((NZ, NY, 16, LANE), BF),
            pltpu.VMEM((NZ, NY, 16, LANE), BF),
            pltpu.VMEM((NZ, NY, 16, LANE), BF),
            pltpu.VMEM((NZ, NY, 16, LANE), BF),
            pltpu.VMEM((NZ, NY, 16, LANE), BF),
            pltpu.VMEM((NZ, NY, 16, DF), BF),
            pltpu.VMEM((PARTS, ROWS, DF), BF),
            pltpu.VMEM((PARTS, ROWS, DF), BF),
            pltpu.VMEM((PARTS, ROWS, WP), BF),
            pltpu.VMEM((PARTS, 64, WP), BF),
            pltpu.VMEM((PARTS, 64, WP), BF),
            pltpu.VMEM((PARTS, 2, BLK, HALF), BF),
            pltpu.VMEM((PARTS, 2, BLK, WP), BF),
            pltpu.VMEM((PARTS, ROWS, WA), BF),
            pltpu.VMEM((PARTS, 2, NY, 16, DF), BF),
            pltpu.VMEM((NZ, NY, 16, CUT), BF),
            pltpu.VMEM((PARTS, NY, 2, 16, DF - CUT), BF),
            pltpu.VMEM((NY, 16, CUT), BF),
            pltpu.VMEM((NY, 16, CUT), BF),
            pltpu.VMEM((NZ, 16, DF - CUT), BF),
            pltpu.VMEM((NZ, 16, DF - CUT), BF),
            pltpu.VMEM((NY, 16, LANE), BF),
            pltpu.VMEM((NZ, 16, LANE), BF),
            dma, dma, dma, dma, dma, dma, dma, dma, dma, dma,
            dma((4, 2)), dma((4, 2)), dma((3, 2)), dma((3, 2)),
            dma, dma, dma, dma,
            dma, dma((NZ,)), dma, dma((PARTS,)), dma, dma, dma, dma,
            dma((PARTS,)), dma((PARTS,)),
            dma((PARTS,)), dma((PARTS, 2)), dma((PARTS, 2)),
            dma((PARTS,)), dma((PARTS, 2)), dma((PARTS, 2)),
            dma((PARTS,)), dma((PARTS,)),
        ],
        compiler_params=pltpu.CompilerParams(
            collective_id=0, has_side_effects=True, vmem_limit_bytes=56 * 1024 * 1024
        ),
    )(
        tokens, expert_ids.T, route_weight.T, grad_mixed, placement, gate_up_base[0], down_base[0],
        gate_up_a[0], gate_up_b[0], down_a[0].T, down_b[0],
    )
    mixed, gtok, gga, ggb, gda, gdb = hand_over(out[:6])
    return mixed, gtok, gga[None], ggb[None], gda.T[None], gdb[None], out[6], out[7]


def solution(mesh):
    return jax.shard_map(
        per_device,
        mesh=mesh,
        in_specs=(
            P("expert", "dp"),
            P("expert", None),
            P("expert", None),
            P(),
            P("expert", "dp", None),
            P("expert", None, "dp"),
            P("expert", "dp", None),
            P("expert", None, None),
            P("expert", None, None),
            P("expert", None, "dp"),
            P("expert", "dp"),
        ),
        out_specs=(
            P("expert", "dp"),
            P("expert", "dp"),
            P("expert", "dp", None),
            P("expert", None, None),
            P("expert", None, None),
            P("expert", None, "dp"),
            P("expert"),
            P("expert"),
        ),
        check_vma=False,
    )
```
